32 devices in a mesh: groups: 2 (over y), ctx: 4 (over z), mp: 4 (over x, core).
Axes of the slice: x: 2, y: 2, z: 4, core: 2. Of those that a mesh axis runs over, the one named last changes fastest.
Arguments:
- block_entry_input: bfloat16 [1536, 2048], P('mp', ('groups', 'ctx')), parts along dimension 1, may hold values from -6 to 6
- first_conv_taps: bfloat16 [3, 768, 1536], P(None, 'mp'), may hold values from -0.09375 to 0.09375
- first_pointwise_weight: bfloat16 [1536, 768], P(None, 'mp'), may hold values from -0.21875 to 0.21875
- second_conv_taps: bfloat16 [3, 768, 1536], P(None, 'mp'), may hold values from -0.09375 to 0.09375
- second_pointwise_weight: bfloat16 [1536, 768], P(None, 'mp'), may hold values from -0.21875 to 0.21875
- grad_heads: bfloat16 [8, 192, 2048], P('mp', 'ctx', 'groups'), parts along dimension 2, may hold values from -6 to 6
Outputs:
- second_block_output: bfloat16 [1536, 2048], P('mp', ('groups', 'ctx')), parts along dimension 1
- entry_input_gradient: bfloat16 [1536, 2048], P('mp', ('groups', 'ctx')), parts along dimension 1
- first_taps_gradient: float32 [6, 768, 1536], P('groups', 'mp', 'ctx'), parts along dimension 0
- first_projection_gradient: float32 [3072, 768], P(('groups', 'ctx'), 'mp'), parts along dimension 0
- second_taps_gradient: float32 [6, 768, 1536], P('groups', 'mp', 'ctx'), parts along dimension 0
- second_projection_gradient: float32 [3072, 768], P(('groups', 'ctx'), 'mp'), parts along dimension 0
The draws below stay inside these ranges and needn't reach their ends.
There are 2 independent parts, one for each index of `groups`. The reference program is written for one: setup_inputs(seed, part) draws one part's arguments, and reference() takes and returns one part's arrays. A program takes and returns all parts, laid end to end along the dimension named above; an argument that names none is the same for every part. Nothing has to cross between parts.
All inputs are finite; a program needn't handle non-finite values.
Results may differ from the reference program's by a relative error of at most 0.034.
Values may be sent and summed in bfloat16 or wider, within the bound.
A program may use at most 192 MiB of HBM per device.

```python
import jax
import jax.numpy as jnp

HEADS = 8
VAL = 192
H = 768
FIRST_DILATION = 1024
SECOND_DILATION = 2048
C = 1536
BINS = 1024


def raised(values, stream_key, source, target, parts, factor):
    def block_of(dim):
        return (jnp.arange(values.shape[dim]) // (values.shape[dim] // parts)).reshape((-1,) + (1,) * (values.ndim - 1 - dim))

    first = jax.random.permutation(stream_key, parts)[block_of(target)]
    other_side = (block_of(target) + parts // 2) % parts
    return jnp.where((block_of(source) == first) | (block_of(source) == other_side), factor * values, values)


def level_of(stream_key, shape, pieces, low, high):
    def one(axis_at, shards_of):
        draws = jax.random.uniform(jax.random.fold_in(jax.random.fold_in(stream_key, 6), axis_at), (shards_of,), jnp.float32, low / len(pieces), high / len(pieces))
        return jnp.repeat(jnp.exp(draws), shape[axis_at] // shards_of).reshape((-1,) + (1,) * (len(shape) - axis_at - 1))

    level = one(*pieces[0])
    for cut in pieces[1:]:
        level = level * one(*cut)
    return level


def normal_values(key, extent, deviation, limit, cuts=(), dtype=jnp.bfloat16):
    values = jax.random.normal(key, extent, jnp.float32) * deviation
    if len(cuts) > 0:
        values = level_of(key, extent, cuts, -0.22, 0.18) * values
    return jnp.clip(values, min=-limit, max=limit).astype(dtype)


def noise_with(stream_key, extent, deviation, reach, cuts, heavy, dtype=jnp.bfloat16):
    array = deviation * jax.random.normal(stream_key, extent, jnp.float32)
    if cuts:
        array = array * level_of(stream_key, extent, cuts, -0.22, 0.18)
    return jnp.clip(raised(array, jax.random.fold_in(stream_key, 3), *heavy), -reach, reach).astype(dtype)


def setup_inputs(seed: int = 0, part: int = 0) -> dict:
    streams_of = jax.random.split(jax.random.key(seed), 7)
    part_splits = jax.random.split(jax.random.fold_in(streams_of[6], part), 7)
    block_entry_input = noise_with(part_splits[0], (C, BINS), 1.0, 6.0, ((0, 4), (1, 4)), (1, 0, 4, 2.0))
    first_conv_taps = normal_values(streams_of[1], (3, H, C), (3 * C) ** -0.5, 0.09375, ((1, 4),))
    first_pointwise_weight = normal_values(streams_of[2], (C, H), H ** -0.5, 0.21875, ((1, 4),))
    second_conv_taps = normal_values(streams_of[3], (3, H, C), (3 * C) ** -0.5, 0.09375, ((1, 4),))
    second_pointwise_weight = normal_values(streams_of[4], (C, H), H ** -0.5, 0.21875, ((1, 4),))
    grad_heads = normal_values(part_splits[5], (HEADS, VAL, BINS), 1.0, 6.0, ((0, 4), (1, 4)))
    return dict(block_entry_input=block_entry_input, first_conv_taps=first_conv_taps, first_pointwise_weight=first_pointwise_weight, second_conv_taps=second_conv_taps, second_pointwise_weight=second_pointwise_weight, grad_heads=grad_heads)


def gelu_slope(values):
    return jax.jvp(jax.nn.gelu, (values,), (jnp.ones_like(values),))[1]


def displaced(field, offset):
    width = field.shape[1]
    margin = abs(offset)
    padded = jnp.pad(field, ((0, 0), (margin, margin)))
    return padded[:, margin + offset: margin + offset + width]


def residual_block_forward(activations, conv_weight, point_weight, dilation):
    squashed = jax.nn.gelu(activations.astype(jnp.float32)).astype(jnp.bfloat16)
    pre_act = jnp.zeros((conv_weight.shape[1], activations.shape[1]), jnp.float32)
    for position in range(3):
        pre_act = pre_act + jnp.dot(conv_weight[position], displaced(squashed, (position - 1) * dilation), preferred_element_type=jnp.float32)
    hidden = jax.nn.gelu(pre_act).astype(jnp.bfloat16)
    mixed = jnp.dot(point_weight, hidden, preferred_element_type=jnp.float32)
    result = (activations.astype(jnp.float32) + mixed).astype(jnp.bfloat16)
    return result, squashed, pre_act, hidden


def residual_block_backward(incoming_gradient, activations, squashed, pre_act, hidden, conv_weight, point_weight, dilation):
    grad_hidden = jnp.dot(point_weight.T, incoming_gradient, preferred_element_type=jnp.float32)
    grad_pre = (grad_hidden * gelu_slope(pre_act)).astype(jnp.bfloat16)
    moved = [displaced(grad_pre, -(position - 1) * dilation) for position in range(3)]
    grad_conv = jnp.stack([jnp.dot(moved[position], squashed.T, preferred_element_type=jnp.float32) for position in range(3)])
    grad_point = jnp.dot(incoming_gradient, hidden.T, preferred_element_type=jnp.float32)
    grad_squash = jnp.zeros((conv_weight.shape[2], incoming_gradient.shape[1]), jnp.float32)
    for position in range(3):
        grad_squash = grad_squash + jnp.dot(conv_weight[position].T, moved[position], preferred_element_type=jnp.float32)
    previous = (incoming_gradient.astype(jnp.float32) + grad_squash * gelu_slope(activations.astype(jnp.float32))).astype(jnp.bfloat16)
    return previous, grad_conv, grad_point


def reference(block_entry_input, first_conv_taps, first_pointwise_weight, second_conv_taps, second_pointwise_weight, grad_heads):
    between_blocks_state, first_gelu_output, first_preactivation, first_hidden_state = residual_block_forward(block_entry_input, first_conv_taps, first_pointwise_weight, FIRST_DILATION)
    second_block_output, second_gelu_output, second_preactivation, second_hidden_state = residual_block_forward(between_blocks_state, second_conv_taps, second_pointwise_weight, SECOND_DILATION)
    incoming_gradient = grad_heads.reshape(HEADS * VAL, BINS)
    incoming_gradient, second_taps_gradient, second_projection_gradient = residual_block_backward(incoming_gradient, between_blocks_state, second_gelu_output, second_preactivation, second_hidden_state, second_conv_taps, second_pointwise_weight, SECOND_DILATION)
    entry_input_gradient, first_taps_gradient, first_projection_gradient = residual_block_backward(incoming_gradient, block_entry_input, first_gelu_output, first_preactivation, first_hidden_state, first_conv_taps, first_pointwise_weight, FIRST_DILATION)
    return second_block_output, entry_input_gradient, first_taps_gradient, first_projection_gradient, second_taps_gradient, second_projection_gradient
```

```python
import functools

import jax
import jax.numpy as jnp
from jax import lax
from jax.experimental import pallas as pl
from jax.experimental.pallas import tpu as pltpu
from jax.sharding import PartitionSpec as P

FIRST_DILATION = 1024
SECOND_DILATION = 2048


def shifted(value, axis, by):
    length = lax.axis_size(axis)
    pairs = [(i, i + by) for i in range(length) if 0 <= i + by < length]
    return lax.ppermute(value, axis, pairs)


def gelu_slope(values):
    return jax.jvp(jax.nn.gelu, (values,), (jnp.ones_like(values),))[1]


def contract_first(left, right):
    return lax.dot_general(
        left, right, (((0,), (0,)), ((), ())), preferred_element_type=jnp.float32
    )


def contract_last(left, right):
    return lax.dot_general(
        left, right, (((1,), (1,)), ((), ())), preferred_element_type=jnp.float32
    )


def hop_steps(activations, dilation):
    return dilation // activations.shape[1]


def residual_block_forward(activations, conv_weight, point_weight, dilation):
    hop_count = hop_steps(activations, dilation)
    squash_part = jax.nn.gelu(activations.astype(jnp.float32)).astype(jnp.bfloat16)
    squashed = lax.all_gather(squash_part, "mp", axis=0, tiled=True)
    earlier = shifted(squashed, "ctx", hop_count)
    later = shifted(squashed, "ctx", -hop_count)
    pre_act = jnp.dot(conv_weight[0], earlier, preferred_element_type=jnp.float32)
    pre_act = pre_act + jnp.dot(conv_weight[1], squashed, preferred_element_type=jnp.float32)
    pre_act = pre_act + jnp.dot(conv_weight[2], later, preferred_element_type=jnp.float32)
    hidden = jax.nn.gelu(pre_act).astype(jnp.bfloat16)
    mixed = lax.psum_scatter(
        jnp.dot(point_weight, hidden, preferred_element_type=jnp.float32).astype(jnp.bfloat16),
        "mp",
        scatter_dimension=0,
        tiled=True,
    ).astype(jnp.float32)
    result = (activations.astype(jnp.float32) + mixed).astype(jnp.bfloat16)
    return (result, squashed, pre_act, hidden)


def residual_block_backward(
    incoming_gradient, activations, squashed, pre_act, hidden, conv_weight, point_weight, dilation
):
    hop_count = hop_steps(activations, dilation)
    upstream_full = lax.all_gather(incoming_gradient, "mp", axis=0, tiled=True)
    grad_hidden = contract_first(point_weight, upstream_full)
    grad_pre = (grad_hidden * gelu_slope(pre_act)).astype(jnp.bfloat16)
    grad_later = shifted(grad_pre, "ctx", -hop_count)
    grad_earlier = shifted(grad_pre, "ctx", hop_count)
    moved = (grad_later, grad_pre, grad_earlier)
    grad_conv = jnp.stack(
        [
            contract_last(moved[0], squashed),
            contract_last(moved[1], squashed),
            contract_last(moved[2], squashed),
        ]
    )
    grad_point = contract_last(upstream_full, hidden)
    total = contract_first(conv_weight[0], moved[0])
    total = total + contract_first(conv_weight[1], moved[1])
    grad_squash = lax.psum_scatter(
        (total + contract_first(conv_weight[2], moved[2])).astype(jnp.bfloat16),
        "mp",
        scatter_dimension=0,
        tiled=True,
    ).astype(jnp.float32)
    previous = (
        incoming_gradient.astype(jnp.float32)
        + grad_squash * gelu_slope(activations.astype(jnp.float32))
    ).astype(jnp.bfloat16)
    return (previous, grad_conv, grad_point)


def reduce_block(grad_conv, grad_point):
    return (
        lax.psum_scatter(
            grad_conv.astype(jnp.bfloat16), "ctx", scatter_dimension=2, tiled=True
        ).astype(jnp.float32),
        lax.psum_scatter(
            grad_point.astype(jnp.bfloat16), "ctx", scatter_dimension=0, tiled=True
        ).astype(jnp.float32),
    )


def shards(
    block_entry_input,
    first_conv_taps,
    first_pointwise_weight,
    second_conv_taps,
    second_pointwise_weight,
    grad_heads,
):
    regrouped = lax.all_to_all(grad_heads, "ctx", split_axis=2, concat_axis=1, tiled=True)
    incoming_gradient = regrouped.reshape(
        regrouped.shape[0] * regrouped.shape[1], regrouped.shape[2]
    )
    between_blocks_state, first_gelu_output, first_preactivation, first_hidden_state = (
        residual_block_forward(
            block_entry_input, first_conv_taps, first_pointwise_weight, FIRST_DILATION
        )
    )
    second_block_output, second_gelu_output, second_preactivation, second_hidden_state = (
        residual_block_forward(
            between_blocks_state, second_conv_taps, second_pointwise_weight, SECOND_DILATION
        )
    )
    incoming_gradient, conv_grad_b, point_grad_b = residual_block_backward(
        incoming_gradient,
        between_blocks_state,
        second_gelu_output,
        second_preactivation,
        second_hidden_state,
        second_conv_taps,
        second_pointwise_weight,
        SECOND_DILATION,
    )
    conv_grad_b, point_grad_b = reduce_block(conv_grad_b, point_grad_b)
    entry_input_gradient, conv_grad_a, point_grad_a = residual_block_backward(
        incoming_gradient,
        block_entry_input,
        first_gelu_output,
        first_preactivation,
        first_hidden_state,
        first_conv_taps,
        first_pointwise_weight,
        FIRST_DILATION,
    )
    conv_grad_a, point_grad_a = reduce_block(conv_grad_a, point_grad_a)
    return (
        second_block_output,
        entry_input_gradient,
        conv_grad_a,
        point_grad_a,
        conv_grad_b,
        point_grad_b,
    )


GELU_SCALE = 0.7978845608028654
GELU_CUBIC = 0.044715


def gelu_of(s):
    return 0.5 * s * (1.0 + jnp.tanh(GELU_SCALE * (s + GELU_CUBIC * (s * s * s))))


def slope_of(s):
    t = jnp.tanh(GELU_SCALE * (s + GELU_CUBIC * (s * s * s)))
    inner = GELU_SCALE * (1.0 + 3.0 * GELU_CUBIC * (s * s))
    return 0.5 * (1.0 + t) + 0.5 * s * (1.0 - t * t) * inner


def whole_kernel(
    n,
    x_h, k1_h, p1_h, k2_h, p2_h, g_h,
    out_o, gx_o, gk1_o, gp1_o, gk2_o, gp2_o,
    x_v, mid_v, k1, p1, k2, p2, z1, z2, g2, g1, u1, u2, v1, v2, gu1, gu2, gh,
    rs_out, rs_in, part, from_left, from_right,
    send, recv, load,
):
    rows, bins = x_v.shape
    chans = z1.shape[0]
    heads, vals = g_h.shape[0], g_h.shape[1]
    c, m = lax.axis_index("ctx"), lax.axis_index("mp")
    sib = m + 1 - 2 * (m % 2)
    cross = (m + 2) % 4
    far = 3 - m
    f32, bf16 = jnp.float32, jnp.bfloat16
    counter = iter(range(send.shape[0]))
    sent = []

    def remote(src, dst, i, **device):
        return pltpu.make_async_remote_copy(
            src_ref=src,
            dst_ref=dst,
            send_sem=send.at[i],
            recv_sem=recv.at[i],
            device_id=device,
            device_id_type=pl.DeviceIdType.MESH,
        )

    def start(copy):
        copy.start()
        sent.append(copy)

    loads = [
        pltpu.make_async_copy(src, dst, load.at[i])
        for i, (src, dst) in enumerate(
            ((x_h, x_v), (k1_h.at[1], k1), (p1_h, p1), (p2_h, p2), (k2_h.at[1], k2))
        )
    ]
    for copy in loads:
        copy.start()

    def grad_rows(owner, h):
        return pl.ds(pl.multiple_of(h * vals * n + owner * vals, 16), vals)

    def grad_bins(owner):
        return pl.ds(pl.multiple_of(owner * bins, 128), bins)

    own_grad = [
        pltpu.make_async_copy(
            g_h.at[h, :, grad_bins(c)], g2.at[m, grad_rows(c, h), :], load.at[5 + h]
        )
        for h in range(heads)
    ]
    for copy in own_grad:
        copy.start()

    barrier = pltpu.get_barrier_semaphore()
    for k in range(1, n):
        pl.semaphore_signal(
            barrier, inc=1, device_id={"ctx": (c + k) % n}, device_id_type=pl.DeviceIdType.MESH
        )
    for peer in (sib, cross):
        pl.semaphore_signal(
            barrier, inc=1, device_id={"mp": peer}, device_id_type=pl.DeviceIdType.MESH
        )

    def gather_start(buf):
        ids = [next(counter) for _ in range(3)]
        start(remote(buf.at[m], buf.at[m], ids[0], mp=cross))
        start(remote(buf.at[m], buf.at[m], ids[1], mp=sib))
        return ids

    def gather_forward(buf, ids):
        remote(buf.at[cross], buf.at[cross], ids[0], mp=cross).wait_recv()
        start(remote(buf.at[cross], buf.at[cross], ids[2], mp=sib))

    def gather_end(buf, ids):
        remote(buf.at[sib], buf.at[sib], ids[1], mp=sib).wait_recv()
        remote(buf.at[far], buf.at[far], ids[2], mp=sib).wait_recv()

    def scatter_start(i, block_of):
        ids = [next(counter) for _ in range(3)]
        for slot, block in ((0, far), (1, sib)):
            rs_out[i, slot] = block_of(block).astype(bf16)
            start(remote(rs_out.at[i, slot], rs_in.at[i, slot], ids[slot], mp=sib))
        return ids

    def scatter_cross(i, ids, block_of):
        term = block_of(cross)
        remote(rs_out.at[i, 0], rs_in.at[i, 0], ids[0], mp=sib).wait_recv()
        rs_out[i, 2] = (term + rs_in[i, 0].astype(f32)).astype(bf16)
        start(remote(rs_out.at[i, 2], rs_in.at[i, 2], ids[2], mp=cross))

    def scatter_end(i, ids, block_of):
        term = block_of(m)
        remote(rs_out.at[i, 1], rs_in.at[i, 1], ids[1], mp=sib).wait_recv()
        term = term + rs_in[i, 1].astype(f32)
        remote(rs_out.at[i, 2], rs_in.at[i, 2], ids[2], mp=cross).wait_recv()
        return term + rs_in[i, 2].astype(f32)

    line_ids = [[(next(counter), next(counter)) for _ in range(n)] for _ in range(4)]

    def to_right(i, d):
        peer = jnp.minimum(c + 1, n - 1)
        return remote(part.at[i, d], from_left.at[i, d], line_ids[i][d][0], ctx=peer)

    def to_left(i, d):
        peer = jnp.maximum(c - 1, 0)
        return remote(part.at[i, d], from_right.at[i, d], line_ids[i][d][1], ctx=peer)

    def line_first(i):
        for d in range(n - 1, 0, -1):

            @pl.when(c == 0)
            def _():
                to_right(i, d).start()

            @pl.when(c == n - 1)
            def _():
                to_left(i, n - 1 - d).start()

    def line_relay(i):
        for d in range(n - 1, 0, -1):

            @pl.when((c > 0) & (c < d))
            def _():
                right = to_right(i, d)
                right.wait_recv()
                part[i, d] = (part[i, d].astype(f32) + from_left[i, d].astype(f32)).astype(bf16)
                right.start()

            @pl.when((c < n - 1) & (c > n - 1 - d))
            def _():
                e = n - 1 - d
                left = to_left(i, e)
                left.wait_recv()
                part[i, e] = (part[i, e].astype(f32) + from_right[i, e].astype(f32)).astype(bf16)
                left.start()

    def line_end(i, result):
        for d in range(n):

            @pl.when(c == d)
            def _():
                total = part[i, d].astype(f32)
                if d > 0:
                    to_right(i, d).wait_recv()
                    total = total + from_left[i, d].astype(f32)
                if d < n - 1:
                    to_left(i, d).wait_recv()
                    total = total + from_right[i, d].astype(f32)
                result[...] = total

    def line_drain(i):
        for d in range(n):

            @pl.when(c < d)
            def _():
                to_right(i, d).wait_send()

            @pl.when(c > d)
            def _():
                to_left(i, d).wait_send()

    def dot(a, b, left, right):
        return lax.dot_general(
            a, b, (((left,), (right,)), ((), ())), preferred_element_type=f32
        )

    def block_rows(b):
        return pl.ds(pl.multiple_of(b * rows, 128), rows)

    def mixed(p, v):
        return lambda b: dot(p[block_rows(b), :], v[...], 1, 0)

    def spread(k, gu):
        return lambda b: dot(k[:, block_rows(b)], gu[...], 0, 0)

    def flat(buf):
        return buf[...].reshape(chans * rows, bins)

    def products(i, left, right):
        for d in range(n):
            part[i, d] = dot(left[...], right[d], 1, 1).astype(bf16)

    loads[0].wait()
    z1[m] = gelu_of(x_v[...].astype(f32)).astype(bf16)
    pl.semaphore_wait(barrier, n + 1)
    z1_ids = gather_start(z1)
    grad_ids = [[next(counter) for _ in range(heads)] for _ in range(n)]
    for k in range(1, n):
        peer = (c + k) % n
        for h in range(heads):
            start(
                remote(
                    g_h.at[h, :, grad_bins(peer)],
                    g2.at[m, grad_rows(c, h), :],
                    grad_ids[k][h],
                    ctx=peer,
                )
            )
    gather_forward(z1, z1_ids)
    for copy in loads[1:]:
        copy.wait()
    gather_end(z1, z1_ids)
    u1[...] = dot(k1[...], flat(z1), 1, 0)
    v1[...] = gelu_of(u1[...]).astype(bf16)
    mixed1 = mixed(p1, v1)
    rs_ids = scatter_start(0, mixed1)
    for copy in own_grad:
        copy.wait()
    for k in range(1, n):
        origin = (c + n - k) % n
        for h in range(heads):
            remote(
                g_h.at[h, :, grad_bins(origin)],
                g2.at[m, grad_rows(origin, h), :],
                grad_ids[k][h],
                ctx=origin,
            ).wait_recv()
    g2_ids = gather_start(g2)
    scatter_cross(0, rs_ids, mixed1)
    gather_forward(g2, g2_ids)
    middle = x_v[...].astype(f32) + scatter_end(0, rs_ids, mixed1)
    mid_v[...] = middle.astype(bf16)
    z2[m] = gelu_of(mid_v[...].astype(f32)).astype(bf16)
    z2_ids = gather_start(z2)
    gather_end(g2, g2_ids)
    gh[...] = dot(p2[...], flat(g2), 0, 0)
    gather_forward(z2, z2_ids)
    gather_end(z2, z2_ids)
    u2[...] = dot(k2[...], flat(z2), 1, 0)
    v2[...] = gelu_of(u2[...]).astype(bf16)
    gu2[...] = (gh[...] * slope_of(u2[...])).astype(bf16)
    spread2 = spread(k2, gu2)
    rs_ids = scatter_start(1, spread2)
    products(0, v2, g2)
    line_first(0)
    scatter_cross(1, rs_ids, spread2)
    products(1, gu2, z2)
    line_first(1)
    mid_slope = slope_of(mid_v[...].astype(f32))
    previous = g2[m].astype(f32) + scatter_end(1, rs_ids, spread2) * mid_slope
    g1[m] = previous.astype(bf16)
    g1_ids = gather_start(g1)
    mixed2 = mixed(p2, v2)
    out_ids = scatter_start(2, mixed2)
    line_relay(0)
    gather_forward(g1, g1_ids)
    gather_end(g1, g1_ids)
    gh[...] = dot(p1[...], flat(g1), 0, 0)
    gu1[...] = (gh[...] * slope_of(u1[...])).astype(bf16)
    spread1 = spread(k1, gu1)
    rs_ids = scatter_start(3, spread1)
    products(2, gu1, z1)
    line_first(2)
    products(3, v1, g1)
    line_first(3)
    scatter_cross(3, rs_ids, spread1)
    scatter_cross(2, out_ids, mixed2)
    line_relay(1)
    first_slope = slope_of(x_v[...].astype(f32))
    previous = g1[m].astype(f32) + scatter_end(3, rs_ids, spread1) * first_slope
    gx_o[...] = previous.astype(bf16)
    result = mid_v[...].astype(f32) + scatter_end(2, out_ids, mixed2)
    out_o[...] = result.astype(bf16)
    line_relay(2)
    line_relay(3)
    for i, result_o in enumerate((gp2_o, gk2_o, gk1_o, gp1_o)):
        line_end(i, result_o)
    for copy in sent:
        copy.wait_send()
    for i in range(4):
        line_drain(i)


def short_sequence(sizes, x, k1, p1, k2, p2, grad):
    n, parts = sizes["ctx"], sizes["mp"]
    rows, bins = x.shape
    width = k1.shape[1]
    bf16, f32 = jnp.bfloat16, jnp.float32
    full = pltpu.VMEM((parts, rows, bins), bf16)
    shares = pltpu.VMEM((4, n, width, rows), bf16)
    copies = 24 + 8 * n + grad.shape[0] * n
    inner = [pltpu.VMEM((width, bins), f32)] * 2 + [pltpu.VMEM((width, bins), bf16)] * 4
    results = pl.pallas_call(
        functools.partial(whole_kernel, n),
        out_shape=[
            jax.ShapeDtypeStruct((rows, bins), bf16),
            jax.ShapeDtypeStruct((rows, bins), bf16),
        ]
        + [jax.ShapeDtypeStruct((width, rows), f32)] * 4,
        in_specs=[pl.BlockSpec(memory_space=pl.ANY)] * 6,
        out_specs=[pl.BlockSpec(memory_space=pltpu.VMEM)] * 6,
        scratch_shapes=[
            pltpu.VMEM((rows, bins), bf16),
            pltpu.VMEM((rows, bins), bf16),
            pltpu.VMEM((width, k1.shape[2]), bf16),
            pltpu.VMEM(p1.shape, bf16),
            pltpu.VMEM((width, k1.shape[2]), bf16),
            pltpu.VMEM(p1.shape, bf16),
            full, full, full, full,
        ]
        + inner
        + [
            pltpu.VMEM((width, bins), f32),
            pltpu.VMEM((4, 3, rows, bins), bf16),
            pltpu.VMEM((4, 3, rows, bins), bf16),
            shares, shares, shares,
            pltpu.SemaphoreType.DMA((copies,)),
            pltpu.SemaphoreType.DMA((copies,)),
            pltpu.SemaphoreType.DMA((5 + grad.shape[0],)),
        ],
        compiler_params=pltpu.CompilerParams(
            collective_id=0, has_side_effects=True, vmem_limit_bytes=48 * 1024 * 1024
        ),
        name="blocks",
    )(x, k1, p1, k2, p2, grad)
    out, gx, gk1, gp1, gk2, gp2 = results
    around = ((1, 1), (0, 0), (0, 0))
    return (
        out,
        gx,
        jnp.pad(gk1[None], around),
        gp1.T,
        jnp.pad(gk2[None], around),
        gp2.T,
    )


def device_program(sizes, x, k1, p1, k2, p2, grad):
    n = sizes["ctx"]
    length = n * x.shape[1]
    short = min(FIRST_DILATION, SECOND_DILATION) >= length
    if short and n == 4 and sizes["mp"] == 4:
        return short_sequence(sizes, x, k1, p1, k2, p2, grad)
    return shards(x, k1, p1, k2, p2, grad)


def solution(mesh):
    placed = (
        P("mp", ("groups", "ctx")),
        P(None, "mp", None),
        P(None, "mp"),
        P(None, "mp", None),
        P(None, "mp"),
        P("mp", "ctx", "groups"),
    )
    return jax.shard_map(
        functools.partial(device_program, dict(mesh.shape)),
        mesh=mesh,
        in_specs=placed,
        out_specs=(
            P("mp", ("groups", "ctx")),
            P("mp", ("groups", "ctx")),
            P("groups", "mp", "ctx"),
            P(("groups", "ctx"), "mp"),
            P("groups", "mp", "ctx"),
            P(("groups", "ctx"), "mp"),
        ),
        check_vma=False,
    )
```

```python
import functools

import jax
import jax.numpy as jnp
from jax import lax
from jax.experimental import pallas as pl
from jax.experimental.pallas import tpu as pltpu
from jax.sharding import PartitionSpec as P

FIRST_DILATION = 1024
SECOND_DILATION = 2048


def shifted(value, axis, by):
    length = lax.axis_size(axis)
    pairs = [(i, i + by) for i in range(length) if 0 <= i + by < length]
    return lax.ppermute(value, axis, pairs)


def gelu_slope(values):
    return jax.jvp(jax.nn.gelu, (values,), (jnp.ones_like(values),))[1]


def contract_first(left, right):
    return lax.dot_general(
        left, right, (((0,), (0,)), ((), ())), preferred_element_type=jnp.float32
    )


def contract_last(left, right):
    return lax.dot_general(
        left, right, (((1,), (1,)), ((), ())), preferred_element_type=jnp.float32
    )


def hop_steps(activations, dilation):
    return dilation // activations.shape[1]


def residual_block_forward(activations, conv_weight, point_weight, dilation):
    hop_count = hop_steps(activations, dilation)
    squash_part = jax.nn.gelu(activations.astype(jnp.float32)).astype(jnp.bfloat16)
    squashed = lax.all_gather(squash_part, "mp", axis=0, tiled=True)
    earlier = shifted(squashed, "ctx", hop_count)
    later = shifted(squashed, "ctx", -hop_count)
    pre_act = jnp.dot(conv_weight[0], earlier, preferred_element_type=jnp.float32)
    pre_act = pre_act + jnp.dot(conv_weight[1], squashed, preferred_element_type=jnp.float32)
    pre_act = pre_act + jnp.dot(conv_weight[2], later, preferred_element_type=jnp.float32)
    hidden = jax.nn.gelu(pre_act).astype(jnp.bfloat16)
    mixed = lax.psum_scatter(
        jnp.dot(point_weight, hidden, preferred_element_type=jnp.float32).astype(jnp.bfloat16),
        "mp",
        scatter_dimension=0,
        tiled=True,
    ).astype(jnp.float32)
    result = (activations.astype(jnp.float32) + mixed).astype(jnp.bfloat16)
    return (result, squashed, pre_act, hidden)


def residual_block_backward(
    incoming_gradient, activations, squashed, pre_act, hidden, conv_weight, point_weight, dilation
):
    hop_count = hop_steps(activations, dilation)
    upstream_full = lax.all_gather(incoming_gradient, "mp", axis=0, tiled=True)
    grad_hidden = contract_first(point_weight, upstream_full)
    grad_pre = (grad_hidden * gelu_slope(pre_act)).astype(jnp.bfloat16)
    grad_later = shifted(grad_pre, "ctx", -hop_count)
    grad_earlier = shifted(grad_pre, "ctx", hop_count)
    moved = (grad_later, grad_pre, grad_earlier)
    grad_conv = jnp.stack(
        [
            contract_last(moved[0], squashed),
            contract_last(moved[1], squashed),
            contract_last(moved[2], squashed),
        ]
    )
    grad_point = contract_last(upstream_full, hidden)
    total = contract_first(conv_weight[0], moved[0])
    total = total + contract_first(conv_weight[1], moved[1])
    grad_squash = lax.psum_scatter(
        (total + contract_first(conv_weight[2], moved[2])).astype(jnp.bfloat16),
        "mp",
        scatter_dimension=0,
        tiled=True,
    ).astype(jnp.float32)
    previous = (
        incoming_gradient.astype(jnp.float32)
        + grad_squash * gelu_slope(activations.astype(jnp.float32))
    ).astype(jnp.bfloat16)
    return (previous, grad_conv, grad_point)


def reduce_block(grad_conv, grad_point):
    return (
        lax.psum_scatter(
            grad_conv.astype(jnp.bfloat16), "ctx", scatter_dimension=2, tiled=True
        ).astype(jnp.float32),
        lax.psum_scatter(
            grad_point.astype(jnp.bfloat16), "ctx", scatter_dimension=0, tiled=True
        ).astype(jnp.float32),
    )


def shards(
    block_entry_input,
    first_conv_taps,
    first_pointwise_weight,
    second_conv_taps,
    second_pointwise_weight,
    grad_heads,
):
    regrouped = lax.all_to_all(grad_heads, "ctx", split_axis=2, concat_axis=1, tiled=True)
    incoming_gradient = regrouped.reshape(
        regrouped.shape[0] * regrouped.shape[1], regrouped.shape[2]
    )
    between_blocks_state, first_gelu_output, first_preactivation, first_hidden_state = (
        residual_block_forward(
            block_entry_input, first_conv_taps, first_pointwise_weight, FIRST_DILATION
        )
    )
    second_block_output, second_gelu_output, second_preactivation, second_hidden_state = (
        residual_block_forward(
            between_blocks_state, second_conv_taps, second_pointwise_weight, SECOND_DILATION
        )
    )
    incoming_gradient, conv_grad_b, point_grad_b = residual_block_backward(
        incoming_gradient,
        between_blocks_state,
        second_gelu_output,
        second_preactivation,
        second_hidden_state,
        second_conv_taps,
        second_pointwise_weight,
        SECOND_DILATION,
    )
    conv_grad_b, point_grad_b = reduce_block(conv_grad_b, point_grad_b)
    entry_input_gradient, conv_grad_a, point_grad_a = residual_block_backward(
        incoming_gradient,
        block_entry_input,
        first_gelu_output,
        first_preactivation,
        first_hidden_state,
        first_conv_taps,
        first_pointwise_weight,
        FIRST_DILATION,
    )
    conv_grad_a, point_grad_a = reduce_block(conv_grad_a, point_grad_a)
    return (
        second_block_output,
        entry_input_gradient,
        conv_grad_a,
        point_grad_a,
        conv_grad_b,
        point_grad_b,
    )


GELU_SCALE = 0.7978845608028654
GELU_CUBIC = 0.044715


def gelu_of(s):
    return 0.5 * s * (1.0 + jnp.tanh(GELU_SCALE * (s + GELU_CUBIC * (s * s * s))))


def slope_of(s):
    t = jnp.tanh(GELU_SCALE * (s + GELU_CUBIC * (s * s * s)))
    inner = GELU_SCALE * (1.0 + 3.0 * GELU_CUBIC * (s * s))
    return 0.5 * (1.0 + t) + 0.5 * s * (1.0 - t * t) * inner


def whole_kernel(
    n,
    x_h, k1_h, p1_h, k2_h, p2_h, g_h,
    out_o, gx_o, gk1_o, gp1_o, gk2_o, gp2_o,
    x_v, mid_v, k1, p1, k2, p2, z1, z2, g2, g1, u1, u2, v1, v2, gu1, gu2, gh,
    rs_out, rs_in, part, from_left, from_right,
    send, recv, load,
):
    rows, bins = x_v.shape
    chans = z1.shape[0]
    heads, vals = g_h.shape[0], g_h.shape[1]
    c, m = lax.axis_index("ctx"), lax.axis_index("mp")
    sib = m + 1 - 2 * (m % 2)
    cross = (m + 2) % 4
    far = 3 - m
    f32, bf16 = jnp.float32, jnp.bfloat16
    counter = iter(range(send.shape[0]))
    sent = []

    def remote(src, dst, i, **device):
        return pltpu.make_async_remote_copy(
            src_ref=src,
            dst_ref=dst,
            send_sem=send.at[i],
            recv_sem=recv.at[i],
            device_id=device,
            device_id_type=pl.DeviceIdType.MESH,
        )

    def start(copy):
        copy.start()
        sent.append(copy)

    loads = [
        pltpu.make_async_copy(src, dst, load.at[i])
        for i, (src, dst) in enumerate(
            ((x_h, x_v), (k1_h.at[1], k1), (p1_h, p1), (p2_h, p2), (k2_h.at[1], k2))
        )
    ]
    for copy in loads:
        copy.start()

    def grad_rows(owner, h):
        return pl.ds(pl.multiple_of(h * vals * n + owner * vals, 16), vals)

    def grad_bins(owner):
        return pl.ds(pl.multiple_of(owner * bins, 128), bins)

    own_grad = [
        pltpu.make_async_copy(
            g_h.at[h, :, grad_bins(c)], g2.at[m, grad_rows(c, h), :], load.at[5 + h]
        )
        for h in range(heads)
    ]
    for copy in own_grad:
        copy.start()

    barrier = pltpu.get_barrier_semaphore()
    for k in range(1, n):
        pl.semaphore_signal(
            barrier, inc=1, device_id={"ctx": (c + k) % n}, device_id_type=pl.DeviceIdType.MESH
        )
    for peer in (sib, cross):
        pl.semaphore_signal(
            barrier, inc=1, device_id={"mp": peer}, device_id_type=pl.DeviceIdType.MESH
        )

    def gather_start(buf):
        ids = [next(counter) for _ in range(3)]
        start(remote(buf.at[m], buf.at[m], ids[0], mp=cross))
        start(remote(buf.at[m], buf.at[m], ids[1], mp=sib))
        return ids

    def gather_forward(buf, ids):
        remote(buf.at[cross], buf.at[cross], ids[0], mp=cross).wait_recv()
        start(remote(buf.at[cross], buf.at[cross], ids[2], mp=sib))

    def gather_end(buf, ids):
        remote(buf.at[sib], buf.at[sib], ids[1], mp=sib).wait_recv()
        remote(buf.at[far], buf.at[far], ids[2], mp=sib).wait_recv()

    def scatter_start(i, block_of):
        ids = [next(counter) for _ in range(3)]
        for slot, block in ((0, far), (1, sib)):
            rs_out[i, slot] = block_of(block).astype(bf16)
            start(remote(rs_out.at[i, slot], rs_in.at[i, slot], ids[slot], mp=sib))
        return ids

    def scatter_cross(i, ids, block_of):
        term = block_of(cross)
        remote(rs_out.at[i, 0], rs_in.at[i, 0], ids[0], mp=sib).wait_recv()
        rs_out[i, 2] = (term + rs_in[i, 0].astype(f32)).astype(bf16)
        start(remote(rs_out.at[i, 2], rs_in.at[i, 2], ids[2], mp=cross))

    def scatter_end(i, ids, block_of):
        term = block_of(m)
        remote(rs_out.at[i, 1], rs_in.at[i, 1], ids[1], mp=sib).wait_recv()
        term = term + rs_in[i, 1].astype(f32)
        remote(rs_out.at[i, 2], rs_in.at[i, 2], ids[2], mp=cross).wait_recv()
        return term + rs_in[i, 2].astype(f32)

    line_ids = [[(next(counter), next(counter)) for _ in range(n)] for _ in range(4)]

    def to_right(i, d):
        peer = jnp.minimum(c + 1, n - 1)
        return remote(part.at[i, d], from_left.at[i, d], line_ids[i][d][0], ctx=peer)

    def to_left(i, d):
        peer = jnp.maximum(c - 1, 0)
        return remote(part.at[i, d], from_right.at[i, d], line_ids[i][d][1], ctx=peer)

    def line_first(*grads):
        for d in range(n - 1, 0, -1):
            for i in grads:

                @pl.when(c == 0)
                def _():
                    to_right(i, d).start()

                @pl.when(c == n - 1)
                def _():
                    to_left(i, n - 1 - d).start()

    def line_relay(i, hop):
        for d in range(n - 1, hop, -1):

            @pl.when(c == hop)
            def _():
                copy = to_right(i, d)
                copy.wait_recv()
                part[i, d] = (part[i, d].astype(f32) + from_left[i, d].astype(f32)).astype(bf16)
                copy.start()

            @pl.when(c == n - 1 - hop)
            def _():
                e = n - 1 - d
                copy = to_left(i, e)
                copy.wait_recv()
                part[i, e] = (part[i, e].astype(f32) + from_right[i, e].astype(f32)).astype(bf16)
                copy.start()

    def line_end(i, result):
        for d in range(n):

            @pl.when(c == d)
            def _():
                total = part[i, d].astype(f32)
                if d > 0:
                    to_right(i, d).wait_recv()
                    total = total + from_left[i, d].astype(f32)
                if d < n - 1:
                    to_left(i, d).wait_recv()
                    total = total + from_right[i, d].astype(f32)
                result[...] = total

    def line_drain(i):
        for d in range(n):

            @pl.when(c < d)
            def _():
                to_right(i, d).wait_send()

            @pl.when(c > d)
            def _():
                to_left(i, d).wait_send()

    def dot(a, b, left, right):
        return lax.dot_general(
            a, b, (((left,), (right,)), ((), ())), preferred_element_type=f32
        )

    def block_rows(b):
        return pl.ds(pl.multiple_of(b * rows, 128), rows)

    def mixed(p, v):
        return lambda b: dot(p[:, block_rows(b)], v[...], 0, 0)

    def spread(k, gu):
        return lambda b: dot(k[:, block_rows(b)], gu[...], 0, 0)

    def flat(buf):
        return buf[...].reshape(chans * rows, bins)

    def products(i, left, right):
        for d in range(n):
            part[i, d] = dot(left[...], right[d], 1, 1).astype(bf16)

    loads[0].wait()
    z1[m] = gelu_of(x_v[...].astype(f32)).astype(bf16)
    pl.semaphore_wait(barrier, n + 1)
    z1_ids = gather_start(z1)
    grad_ids = [[next(counter) for _ in range(heads)] for _ in range(n)]
    for k in range(1, n):
        peer = (c + k) % n
        for h in range(heads):
            start(
                remote(
                    g_h.at[h, :, grad_bins(peer)],
                    g2.at[m, grad_rows(c, h), :],
                    grad_ids[k][h],
                    ctx=peer,
                )
            )
    gather_forward(z1, z1_ids)
    for copy in loads[1:]:
        copy.wait()
    gather_end(z1, z1_ids)
    u1[...] = dot(k1[...], flat(z1), 1, 0)
    v1[...] = gelu_of(u1[...]).astype(bf16)
    mixed1 = mixed(p1, v1)
    rs_ids = scatter_start(0, mixed1)
    for copy in own_grad:
        copy.wait()
    for k in range(1, n):
        origin = (c + n - k) % n
        for h in range(heads):
            remote(
                g_h.at[h, :, grad_bins(origin)],
                g2.at[m, grad_rows(origin, h), :],
                grad_ids[k][h],
                ctx=origin,
            ).wait_recv()
    g2_ids = gather_start(g2)
    scatter_cross(0, rs_ids, mixed1)
    gather_forward(g2, g2_ids)
    middle = x_v[...].astype(f32) + scatter_end(0, rs_ids, mixed1)
    mid_v[...] = middle.astype(bf16)
    z2[m] = gelu_of(mid_v[...].astype(f32)).astype(bf16)
    z2_ids = gather_start(z2)
    gather_end(g2, g2_ids)
    gh[...] = dot(p2[...], flat(g2), 1, 0)
    gather_forward(z2, z2_ids)
    gather_end(z2, z2_ids)
    u2[...] = dot(k2[...], flat(z2), 1, 0)
    v2[...] = gelu_of(u2[...]).astype(bf16)
    gu2[...] = (gh[...] * slope_of(u2[...])).astype(bf16)
    spread2 = spread(k2, gu2)
    rs_ids = scatter_start(1, spread2)
    products(0, v2, g2)
    products(1, gu2, z2)
    line_first(0, 1)
    scatter_cross(1, rs_ids, spread2)
    mid_slope = slope_of(mid_v[...].astype(f32))
    mixed2 = mixed(p2, v2)
    out_ids = scatter_start(2, mixed2)
    previous = g2[m].astype(f32) + scatter_end(1, rs_ids, spread2) * mid_slope
    g1[m] = previous.astype(bf16)
    g1_ids = gather_start(g1)
    line_relay(0, 1)
    gather_forward(g1, g1_ids)
    gather_end(g1, g1_ids)
    gh[...] = dot(p1[...], flat(g1), 1, 0)
    gu1[...] = (gh[...] * slope_of(u1[...])).astype(bf16)
    spread1 = spread(k1, gu1)
    rs_ids = scatter_start(3, spread1)
    products(2, gu1, z1)
    products(3, v1, g1)
    line_first(2, 3)
    line_relay(1, 1)
    for i in (0, 1):
        for hop in range(2, n - 1):
            line_relay(i, hop)
    scatter_cross(3, rs_ids, spread1)
    scatter_cross(2, out_ids, mixed2)
    first_slope = slope_of(x_v[...].astype(f32))
    previous = g1[m].astype(f32) + scatter_end(3, rs_ids, spread1) * first_slope
    gx_o[...] = previous.astype(bf16)
    result = mid_v[...].astype(f32) + scatter_end(2, out_ids, mixed2)
    out_o[...] = result.astype(bf16)
    for hop in range(1, n - 1):
        for i in (2, 3):
            line_relay(i, hop)
    for i, result_o in enumerate((gp2_o, gk2_o, gk1_o, gp1_o)):
        line_end(i, result_o)
    for copy in sent:
        copy.wait_send()
    for i in range(4):
        line_drain(i)


def write_results(out_i, gx_i, gk1_i, gp1_i, gk2_i, gp2_i, out_o, gx_o, gk1_o, gp1_o, gk2_o, gp2_o):
    for taken, given in ((out_i, out_o), (gx_i, gx_o), (gp1_i, gp1_o), (gp2_i, gp2_o)):
        given[...] = taken[...]
    for taken, given in ((gk1_i, gk1_o), (gk2_i, gk2_o)):
        given[...] = jnp.zeros_like(given)
        given[1] = taken[...]


def short_sequence(sizes, x, k1, p1, k2, p2, grad):
    n, parts = sizes["ctx"], sizes["mp"]
    rows, bins = x.shape
    width = k1.shape[1]
    bf16, f32 = jnp.bfloat16, jnp.float32
    full = pltpu.VMEM((parts, rows, bins), bf16)
    shares = pltpu.VMEM((4, n, width, rows), bf16)
    copies = 24 + 8 * n + grad.shape[0] * n
    inner = [pltpu.VMEM((width, bins), f32)] * 2 + [pltpu.VMEM((width, bins), bf16)] * 4
    results = pl.pallas_call(
        functools.partial(whole_kernel, n),
        out_shape=[
            jax.ShapeDtypeStruct((rows, bins), bf16),
            jax.ShapeDtypeStruct((rows, bins), bf16),
        ]
        + [jax.ShapeDtypeStruct((width, rows), f32)] * 4,
        in_specs=[pl.BlockSpec(memory_space=pl.ANY)] * 6,
        out_specs=[pl.BlockSpec(memory_space=pltpu.VMEM)] * 6,
        scratch_shapes=[
            pltpu.VMEM((rows, bins), bf16),
            pltpu.VMEM((rows, bins), bf16),
            pltpu.VMEM((width, k1.shape[2]), bf16),
            pltpu.VMEM(p1.shape[::-1], bf16),
            pltpu.VMEM((width, k1.shape[2]), bf16),
            pltpu.VMEM(p1.shape[::-1], bf16),
            full, full, full, full,
        ]
        + inner
        + [
            pltpu.VMEM((width, bins), f32),
            pltpu.VMEM((4, 3, rows, bins), bf16),
            pltpu.VMEM((4, 3, rows, bins), bf16),
            shares, shares, shares,
            pltpu.SemaphoreType.DMA((copies,)),
            pltpu.SemaphoreType.DMA((copies,)),
            pltpu.SemaphoreType.DMA((5 + grad.shape[0],)),
        ],
        compiler_params=pltpu.CompilerParams(
            collective_id=0, has_side_effects=True, vmem_limit_bytes=56 * 1024 * 1024
        ),
        name="blocks",
    )(x, k1, p1.T, k2, p2.T, grad)
    taps = jax.ShapeDtypeStruct((k1.shape[0], width, rows), f32)
    points = jax.ShapeDtypeStruct((width, rows), f32)
    out, gx, gk1, gp1, gk2, gp2 = pl.pallas_call(
        write_results,
        out_shape=[
            jax.ShapeDtypeStruct((rows, bins), bf16),
            jax.ShapeDtypeStruct((rows, bins), bf16),
            taps, points, taps, points,
        ],
        in_specs=[pl.BlockSpec(memory_space=pltpu.VMEM)] * 6,
        out_specs=[pl.BlockSpec(memory_space=pltpu.VMEM)] * 6,
        name="results",
    )(*results)
    return out, gx, gk1, gp1.T, gk2, gp2.T


def device_program(sizes, x, k1, p1, k2, p2, grad):
    n = sizes["ctx"]
    length = n * x.shape[1]
    short = min(FIRST_DILATION, SECOND_DILATION) >= length
    if short and n == 4 and sizes["mp"] == 4:
        return short_sequence(sizes, x, k1, p1, k2, p2, grad)
    return shards(x, k1, p1, k2, p2, grad)


def solution(mesh):
    placed = (
        P("mp", ("groups", "ctx")),
        P(None, "mp", None),
        P(None, "mp"),
        P(None, "mp", None),
        P(None, "mp"),
        P("mp", "ctx", "groups"),
    )
    return jax.shard_map(
        functools.partial(device_program, dict(mesh.shape)),
        mesh=mesh,
        in_specs=placed,
        out_specs=(
            P("mp", ("groups", "ctx")),
            P("mp", ("groups", "ctx")),
            P("groups", "mp", "ctx"),
            P(("groups", "ctx"), "mp"),
            P("groups", "mp", "ctx"),
            P(("groups", "ctx"), "mp"),
        ),
        check_vma=False,
    )
```

```python
import functools

import jax
import jax.numpy as jnp
from jax import lax
from jax.experimental import pallas as pl
from jax.experimental.pallas import tpu as pltpu
from jax.sharding import PartitionSpec as P

FIRST_DILATION = 1024
SECOND_DILATION = 2048


def shifted(value, axis, by):
    length = lax.axis_size(axis)
    pairs = [(i, i + by) for i in range(length) if 0 <= i + by < length]
    return lax.ppermute(value, axis, pairs)


def gelu_slope(values):
    return jax.jvp(jax.nn.gelu, (values,), (jnp.ones_like(values),))[1]


def contract_first(left, right):
    return lax.dot_general(
        left, right, (((0,), (0,)), ((), ())), preferred_element_type=jnp.float32
    )


def contract_last(left, right):
    return lax.dot_general(
        left, right, (((1,), (1,)), ((), ())), preferred_element_type=jnp.float32
    )


def hop_steps(activations, dilation):
    return dilation // activations.shape[1]


def residual_block_forward(activations, conv_weight, point_weight, dilation):
    hop_count = hop_steps(activations, dilation)
    squash_part = jax.nn.gelu(activations.astype(jnp.float32)).astype(jnp.bfloat16)
    squashed = lax.all_gather(squash_part, "mp", axis=0, tiled=True)
    earlier = shifted(squashed, "ctx", hop_count)
    later = shifted(squashed, "ctx", -hop_count)
    pre_act = jnp.dot(conv_weight[0], earlier, preferred_element_type=jnp.float32)
    pre_act = pre_act + jnp.dot(conv_weight[1], squashed, preferred_element_type=jnp.float32)
    pre_act = pre_act + jnp.dot(conv_weight[2], later, preferred_element_type=jnp.float32)
    hidden = jax.nn.gelu(pre_act).astype(jnp.bfloat16)
    mixed = lax.psum_scatter(
        jnp.dot(point_weight, hidden, preferred_element_type=jnp.float32).astype(jnp.bfloat16),
        "mp",
        scatter_dimension=0,
        tiled=True,
    ).astype(jnp.float32)
    result = (activations.astype(jnp.float32) + mixed).astype(jnp.bfloat16)
    return (result, squashed, pre_act, hidden)


def residual_block_backward(
    incoming_gradient, activations, squashed, pre_act, hidden, conv_weight, point_weight, dilation
):
    hop_count = hop_steps(activations, dilation)
    upstream_full = lax.all_gather(incoming_gradient, "mp", axis=0, tiled=True)
    grad_hidden = contract_first(point_weight, upstream_full)
    grad_pre = (grad_hidden * gelu_slope(pre_act)).astype(jnp.bfloat16)
    grad_later = shifted(grad_pre, "ctx", -hop_count)
    grad_earlier = shifted(grad_pre, "ctx", hop_count)
    moved = (grad_later, grad_pre, grad_earlier)
    grad_conv = jnp.stack(
        [
            contract_last(moved[0], squashed),
            contract_last(moved[1], squashed),
            contract_last(moved[2], squashed),
        ]
    )
    grad_point = contract_last(upstream_full, hidden)
    total = contract_first(conv_weight[0], moved[0])
    total = total + contract_first(conv_weight[1], moved[1])
    grad_squash = lax.psum_scatter(
        (total + contract_first(conv_weight[2], moved[2])).astype(jnp.bfloat16),
        "mp",
        scatter_dimension=0,
        tiled=True,
    ).astype(jnp.float32)
    previous = (
        incoming_gradient.astype(jnp.float32)
        + grad_squash * gelu_slope(activations.astype(jnp.float32))
    ).astype(jnp.bfloat16)
    return (previous, grad_conv, grad_point)


def reduce_block(grad_conv, grad_point):
    return (
        lax.psum_scatter(
            grad_conv.astype(jnp.bfloat16), "ctx", scatter_dimension=2, tiled=True
        ).astype(jnp.float32),
        lax.psum_scatter(
            grad_point.astype(jnp.bfloat16), "ctx", scatter_dimension=0, tiled=True
        ).astype(jnp.float32),
    )


def shards(
    block_entry_input,
    first_conv_taps,
    first_pointwise_weight,
    second_conv_taps,
    second_pointwise_weight,
    grad_heads,
):
    regrouped = lax.all_to_all(grad_heads, "ctx", split_axis=2, concat_axis=1, tiled=True)
    incoming_gradient = regrouped.reshape(
        regrouped.shape[0] * regrouped.shape[1], regrouped.shape[2]
    )
    between_blocks_state, first_gelu_output, first_preactivation, first_hidden_state = (
        residual_block_forward(
            block_entry_input, first_conv_taps, first_pointwise_weight, FIRST_DILATION
        )
    )
    second_block_output, second_gelu_output, second_preactivation, second_hidden_state = (
        residual_block_forward(
            between_blocks_state, second_conv_taps, second_pointwise_weight, SECOND_DILATION
        )
    )
    incoming_gradient, conv_grad_b, point_grad_b = residual_block_backward(
        incoming_gradient,
        between_blocks_state,
        second_gelu_output,
        second_preactivation,
        second_hidden_state,
        second_conv_taps,
        second_pointwise_weight,
        SECOND_DILATION,
    )
    conv_grad_b, point_grad_b = reduce_block(conv_grad_b, point_grad_b)
    entry_input_gradient, conv_grad_a, point_grad_a = residual_block_backward(
        incoming_gradient,
        block_entry_input,
        first_gelu_output,
        first_preactivation,
        first_hidden_state,
        first_conv_taps,
        first_pointwise_weight,
        FIRST_DILATION,
    )
    conv_grad_a, point_grad_a = reduce_block(conv_grad_a, point_grad_a)
    return (
        second_block_output,
        entry_input_gradient,
        conv_grad_a,
        point_grad_a,
        conv_grad_b,
        point_grad_b,
    )


GELU_SCALE = 0.7978845608028654
GELU_CUBIC = 0.044715


def gelu_of(s):
    return 0.5 * s * (1.0 + jnp.tanh(GELU_SCALE * (s + GELU_CUBIC * (s * s * s))))


def slope_of(s):
    t = jnp.tanh(GELU_SCALE * (s + GELU_CUBIC * (s * s * s)))
    inner = GELU_SCALE * (1.0 + 3.0 * GELU_CUBIC * (s * s))
    return 0.5 * (1.0 + t) + 0.5 * s * (1.0 - t * t) * inner


def whole_kernel(
    n,
    x_h, k1_h, p1_h, k2_h, p2_h, g_h,
    out_o, gx_o, gk1_o, gp1_o, gk2_o, gp2_o,
    x_v, mid_v, k1, p1, k2, p2, z1, z2, g2, g1, u1, u2, gh, v2, gu2,
    v_all, gu_all, z_rows, g_rows,
    rs_out, rs_in, part, from_left, from_right,
    send, recv, load,
):
    rows, bins = x_v.shape
    chans = z1.shape[0]
    heads, vals = g_h.shape[0], g_h.shape[1]
    c, m = lax.axis_index("ctx"), lax.axis_index("mp")
    sib = m + 1 - 2 * (m % 2)
    cross = (m + 2) % 4
    far = 3 - m
    f32, bf16 = jnp.float32, jnp.bfloat16
    counter = iter(range(send.shape[0]))
    sent = []

    def remote(src, dst, i, **device):
        return pltpu.make_async_remote_copy(
            src_ref=src,
            dst_ref=dst,
            send_sem=send.at[i],
            recv_sem=recv.at[i],
            device_id=device,
            device_id_type=pl.DeviceIdType.MESH,
        )

    def start(copy):
        copy.start()
        sent.append(copy)

    loads = [
        pltpu.make_async_copy(src, dst, load.at[i])
        for i, (src, dst) in enumerate(
            ((x_h, x_v), (k1_h.at[1], k1), (p1_h, p1), (p2_h, p2), (k2_h.at[1], k2))
        )
    ]
    for copy in loads:
        copy.start()

    def grad_rows(owner, h):
        return pl.ds(pl.multiple_of(h * vals * n + owner * vals, 16), vals)

    def grad_bins(owner):
        return pl.ds(pl.multiple_of(owner * bins, 128), bins)

    own_grad = [
        pltpu.make_async_copy(
            g_h.at[h, :, grad_bins(c)], g2.at[m, grad_rows(c, h), :], load.at[5 + h]
        )
        for h in range(heads)
    ]
    for copy in own_grad:
        copy.start()

    barrier = pltpu.get_barrier_semaphore()
    for k in range(1, n):
        pl.semaphore_signal(
            barrier, inc=1, device_id={"ctx": (c + k) % n}, device_id_type=pl.DeviceIdType.MESH
        )
    for peer in (sib, cross):
        pl.semaphore_signal(
            barrier, inc=1, device_id={"mp": peer}, device_id_type=pl.DeviceIdType.MESH
        )

    def pieces(buf):
        return [lambda b: buf.at[b]]

    def gather_start(views):
        ids = []
        for view in views:
            own = [next(counter) for _ in range(3)]
            start(remote(view(m), view(m), own[0], mp=cross))
            start(remote(view(m), view(m), own[1], mp=sib))
            ids.append(own)
        return ids

    def gather_forward(views, ids):
        for view, own in zip(views, ids):
            remote(view(cross), view(cross), own[0], mp=cross).wait_recv()
            start(remote(view(cross), view(cross), own[2], mp=sib))

    def gather_end(views, ids):
        for view, own in zip(views, ids):
            remote(view(sib), view(sib), own[1], mp=sib).wait_recv()
            remote(view(far), view(far), own[2], mp=sib).wait_recv()

    def push_start(source, target):
        ids = [next(counter) for _ in range(n)]
        for k in range(1, n):
            peer = (c + k) % n
            start(remote(source(peer), target(c), ids[k], ctx=peer))
        return ids

    def push_wait(target, ids):
        for k in range(1, n):
            origin = (c + n - k) % n
            remote(target(origin), target(origin), ids[k], ctx=origin).wait_recv()

    def quarter(b):
        return pl.ds(pl.multiple_of(b * (rows // 4), 16), rows // 4)

    def row_views(buf):
        def view_of(k):
            return lambda b: buf.at[(c + k) % n, quarter(b), :]

        return [view_of(k) for k in range(1, n)]

    def scatter_start(i, block_of):
        ids = [next(counter) for _ in range(3)]
        for slot, block in ((0, far), (1, sib)):
            rs_out[i, slot] = block_of(block).astype(bf16)
            start(remote(rs_out.at[i, slot], rs_in.at[i, slot], ids[slot], mp=sib))
        return ids

    def scatter_cross(i, ids, block_of):
        term = block_of(cross)
        remote(rs_out.at[i, 0], rs_in.at[i, 0], ids[0], mp=sib).wait_recv()
        rs_out[i, 2] = (term + rs_in[i, 0].astype(f32)).astype(bf16)
        start(remote(rs_out.at[i, 2], rs_in.at[i, 2], ids[2], mp=cross))

    def scatter_end(i, ids, block_of):
        term = block_of(m)
        remote(rs_out.at[i, 1], rs_in.at[i, 1], ids[1], mp=sib).wait_recv()
        term = term + rs_in[i, 1].astype(f32)
        remote(rs_out.at[i, 2], rs_in.at[i, 2], ids[2], mp=cross).wait_recv()
        return term + rs_in[i, 2].astype(f32)

    line_ids = [[(next(counter), next(counter)) for _ in range(n)] for _ in range(2)]

    def to_right(i, d):
        peer = jnp.minimum(c + 1, n - 1)
        return remote(part.at[i, d], from_left.at[i, d], line_ids[i][d][0], ctx=peer)

    def to_left(i, d):
        peer = jnp.maximum(c - 1, 0)
        return remote(part.at[i, d], from_right.at[i, d], line_ids[i][d][1], ctx=peer)

    def line_first(*grads):
        for d in range(n - 1, 0, -1):
            for i in grads:

                @pl.when(c == 0)
                def _():
                    to_right(i, d).start()

                @pl.when(c == n - 1)
                def _():
                    to_left(i, n - 1 - d).start()

    def line_relay(i, hop):
        for d in range(n - 1, hop, -1):

            @pl.when(c == hop)
            def _():
                copy = to_right(i, d)
                copy.wait_recv()
                part[i, d] = (part[i, d].astype(f32) + from_left[i, d].astype(f32)).astype(bf16)
                copy.start()

            @pl.when(c == n - 1 - hop)
            def _():
                e = n - 1 - d
                copy = to_left(i, e)
                copy.wait_recv()
                part[i, e] = (part[i, e].astype(f32) + from_right[i, e].astype(f32)).astype(bf16)
                copy.start()

    def line_end(i, result):
        for d in range(n):

            @pl.when(c == d)
            def _():
                total = part[i, d].astype(f32)
                if d > 0:
                    to_right(i, d).wait_recv()
                    total = total + from_left[i, d].astype(f32)
                if d < n - 1:
                    to_left(i, d).wait_recv()
                    total = total + from_right[i, d].astype(f32)
                result[...] = total

    def line_drain(i):
        for d in range(n):

            @pl.when(c < d)
            def _():
                to_right(i, d).wait_send()

            @pl.when(c > d)
            def _():
                to_left(i, d).wait_send()

    def dot(a, b, left, right):
        return lax.dot_general(
            a, b, (((left,), (right,)), ((), ())), preferred_element_type=f32
        )

    def block_rows(b):
        return pl.ds(pl.multiple_of(b * rows, 128), rows)

    def mixed(p, v):
        return lambda b: dot(p[:, block_rows(b)], v[...], 0, 0)

    def spread(k, gu):
        return lambda b: dot(k[:, block_rows(b)], gu[...], 0, 0)

    def flat(buf):
        return buf[...].reshape(chans * rows, bins)

    def products(i, left, right):
        for d in range(n):
            part[i, d] = dot(left[...], right[d], 1, 1).astype(bf16)

    loads[0].wait()
    z1[m] = gelu_of(x_v[...].astype(f32)).astype(bf16)
    pl.semaphore_wait(barrier, n + 1)
    z1_ids = gather_start(pieces(z1))
    grad_ids = [[next(counter) for _ in range(heads)] for _ in range(n)]
    for k in range(1, n):
        peer = (c + k) % n
        for h in range(heads):
            start(
                remote(
                    g_h.at[h, :, grad_bins(peer)],
                    g2.at[m, grad_rows(c, h), :],
                    grad_ids[k][h],
                    ctx=peer,
                )
            )
    gather_forward(pieces(z1), z1_ids)
    for copy in loads[1:]:
        copy.wait()
    gather_end(pieces(z1), z1_ids)
    u1[...] = dot(k1[...], flat(z1), 1, 0)
    v_all[c] = gelu_of(u1[...]).astype(bf16)
    mixed1 = mixed(p1, v_all.at[c])
    rs_ids = scatter_start(0, mixed1)
    for copy in own_grad:
        copy.wait()
    for k in range(1, n):
        origin = (c + n - k) % n
        for h in range(heads):
            remote(
                g_h.at[h, :, grad_bins(origin)],
                g2.at[m, grad_rows(origin, h), :],
                grad_ids[k][h],
                ctx=origin,
            ).wait_recv()
    g2_ids = gather_start(pieces(g2))
    v_ids = push_start(lambda peer: v_all.at[c], lambda at: v_all.at[at])
    z_ids = push_start(lambda peer: z1.at[peer, quarter(m), :], lambda at: z_rows.at[at, quarter(m), :])
    scatter_cross(0, rs_ids, mixed1)
    gather_forward(pieces(g2), g2_ids)
    middle = x_v[...].astype(f32) + scatter_end(0, rs_ids, mixed1)
    mid_v[...] = middle.astype(bf16)
    z2[m] = gelu_of(mid_v[...].astype(f32)).astype(bf16)
    z2_ids = gather_start(pieces(z2))
    gather_end(pieces(g2), g2_ids)
    gh[...] = dot(p2[...], flat(g2), 1, 0)
    gather_forward(pieces(z2), z2_ids)
    gather_end(pieces(z2), z2_ids)
    u2[...] = dot(k2[...], flat(z2), 1, 0)
    v2[...] = gelu_of(u2[...]).astype(bf16)
    gu2[...] = (gh[...] * slope_of(u2[...])).astype(bf16)
    spread2 = spread(k2, gu2)
    rs_ids = scatter_start(1, spread2)
    products(0, v2, g2)
    products(1, gu2, z2)
    line_first(0, 1)
    scatter_cross(1, rs_ids, spread2)
    mid_slope = slope_of(mid_v[...].astype(f32))
    mixed2 = mixed(p2, v2)
    out_ids = scatter_start(2, mixed2)
    previous = g2[m].astype(f32) + scatter_end(1, rs_ids, spread2) * mid_slope
    g1[m] = previous.astype(bf16)
    g1_ids = gather_start(pieces(g1))
    line_relay(0, 1)
    gather_forward(pieces(g1), g1_ids)
    gather_end(pieces(g1), g1_ids)
    g_ids = push_start(lambda peer: g1.at[peer, quarter(m), :], lambda at: g_rows.at[at, quarter(m), :])
    gh[...] = dot(p1[...], flat(g1), 1, 0)
    gu_all[c] = (gh[...] * slope_of(u1[...])).astype(bf16)
    gu_ids = push_start(lambda peer: gu_all.at[c], lambda at: gu_all.at[at])
    spread1 = spread(k1, gu_all.at[c])
    rs_ids = scatter_start(3, spread1)
    line_relay(1, 1)
    scatter_cross(3, rs_ids, spread1)
    push_wait(lambda at: z_rows.at[at, quarter(m), :], z_ids)
    z_row_ids = gather_start(row_views(z_rows))
    scatter_cross(2, out_ids, mixed2)
    for i in (0, 1):
        for hop in range(2, n - 1):
            line_relay(i, hop)
    first_slope = slope_of(x_v[...].astype(f32))
    previous = g1[m].astype(f32) + scatter_end(3, rs_ids, spread1) * first_slope
    gx_o[...] = previous.astype(bf16)
    gather_forward(row_views(z_rows), z_row_ids)
    push_wait(lambda at: g_rows.at[at, quarter(m), :], g_ids)
    g_row_ids = gather_start(row_views(g_rows))
    result = mid_v[...].astype(f32) + scatter_end(2, out_ids, mixed2)
    out_o[...] = result.astype(bf16)
    gather_end(row_views(z_rows), z_row_ids)
    z_rows[c] = z1[c]
    g_rows[c] = g1[c]
    gather_forward(row_views(g_rows), g_row_ids)
    push_wait(lambda at: gu_all.at[at], gu_ids)
    gk1_o[...] = sum(dot(gu_all[k], z_rows[k], 1, 1) for k in range(n))
    push_wait(lambda at: v_all.at[at], v_ids)
    gather_end(row_views(g_rows), g_row_ids)
    gp1_o[...] = sum(dot(v_all[k], g_rows[k], 1, 1) for k in range(n))
    for i, result_o in enumerate((gp2_o, gk2_o)):
        line_end(i, result_o)
    for copy in sent:
        copy.wait_send()
    for i in range(2):
        line_drain(i)


def write_results(out_i, gx_i, gk1_i, gp1_i, gk2_i, gp2_i, out_o, gx_o, gk1_o, gp1_o, gk2_o, gp2_o):
    for taken, given in ((out_i, out_o), (gx_i, gx_o), (gp1_i, gp1_o), (gp2_i, gp2_o)):
        given[...] = taken[...]
    for taken, given in ((gk1_i, gk1_o), (gk2_i, gk2_o)):
        given[...] = jnp.zeros_like(given)
        given[1] = taken[...]


def short_sequence(sizes, x, k1, p1, k2, p2, grad):
    n, parts = sizes["ctx"], sizes["mp"]
    rows, bins = x.shape
    width = k1.shape[1]
    bf16, f32 = jnp.bfloat16, jnp.float32
    full = pltpu.VMEM((parts, rows, bins), bf16)
    shares = pltpu.VMEM((2, n, width, rows), bf16)
    copies = 24 + 4 * n + 4 * n + 6 * (n - 1) + grad.shape[0] * n
    inner = [pltpu.VMEM((width, bins), f32)] * 3 + [pltpu.VMEM((width, bins), bf16)] * 2
    results = pl.pallas_call(
        functools.partial(whole_kernel, n),
        out_shape=[
            jax.ShapeDtypeStruct((rows, bins), bf16),
            jax.ShapeDtypeStruct((rows, bins), bf16),
        ]
        + [jax.ShapeDtypeStruct((width, rows), f32)] * 4,
        in_specs=[pl.BlockSpec(memory_space=pl.ANY)] * 6,
        out_specs=[pl.BlockSpec(memory_space=pltpu.VMEM)] * 6,
        scratch_shapes=[
            pltpu.VMEM((rows, bins), bf16),
            pltpu.VMEM((rows, bins), bf16),
            pltpu.VMEM((width, k1.shape[2]), bf16),
            pltpu.VMEM(p1.shape[::-1], bf16),
            pltpu.VMEM((width, k1.shape[2]), bf16),
            pltpu.VMEM(p1.shape[::-1], bf16),
            full, full, full, full,
        ]
        + inner
        + [
            pltpu.VMEM((n, width, bins), bf16),
            pltpu.VMEM((n, width, bins), bf16),
            pltpu.VMEM((n, rows, bins), bf16),
            pltpu.VMEM((n, rows, bins), bf16),
            pltpu.VMEM((4, 3, rows, bins), bf16),
            pltpu.VMEM((4, 3, rows, bins), bf16),
            shares, shares, shares,
            pltpu.SemaphoreType.DMA((copies,)),
            pltpu.SemaphoreType.DMA((copies,)),
            pltpu.SemaphoreType.DMA((5 + grad.shape[0],)),
        ],
        compiler_params=pltpu.CompilerParams(
            collective_id=0, has_side_effects=True, vmem_limit_bytes=56 * 1024 * 1024
        ),
        name="blocks",
    )(x, k1, p1.T, k2, p2.T, grad)
    taps = jax.ShapeDtypeStruct((k1.shape[0], width, rows), f32)
    points = jax.ShapeDtypeStruct((width, rows), f32)
    out, gx, gk1, gp1, gk2, gp2 = pl.pallas_call(
        write_results,
        out_shape=[
            jax.ShapeDtypeStruct((rows, bins), bf16),
            jax.ShapeDtypeStruct((rows, bins), bf16),
            taps, points, taps, points,
        ],
        in_specs=[pl.BlockSpec(memory_space=pltpu.VMEM)] * 6,
        out_specs=[pl.BlockSpec(memory_space=pltpu.VMEM)] * 6,
        name="results",
    )(*results)
    return out, gx, gk1, gp1.T, gk2, gp2.T


def device_program(sizes, x, k1, p1, k2, p2, grad):
    n = sizes["ctx"]
    length = n * x.shape[1]
    short = min(FIRST_DILATION, SECOND_DILATION) >= length
    if short and n == 4 and sizes["mp"] == 4:
        return short_sequence(sizes, x, k1, p1, k2, p2, grad)
    return shards(x, k1, p1, k2, p2, grad)


def solution(mesh):
    placed = (
        P("mp", ("groups", "ctx")),
        P(None, "mp", None),
        P(None, "mp"),
        P(None, "mp", None),
        P(None, "mp"),
        P("mp", "ctx", "groups"),
    )
    return jax.shard_map(
        functools.partial(device_program, dict(mesh.shape)),
        mesh=mesh,
        in_specs=placed,
        out_specs=(
            P("mp", ("groups", "ctx")),
            P("mp", ("groups", "ctx")),
            P("groups", "mp", "ctx"),
            P(("groups", "ctx"), "mp"),
            P("groups", "mp", "ctx"),
            P(("groups", "ctx"), "mp"),
        ),
        check_vma=False,
    )
```

```python
import functools

import jax
import jax.numpy as jnp
from jax import lax
from jax.experimental import pallas as pl
from jax.experimental.pallas import tpu as pltpu
from jax.sharding import PartitionSpec as P

FIRST_DILATION = 1024
SECOND_DILATION = 2048


def shifted(value, axis, by):
    length = lax.axis_size(axis)
    pairs = [(i, i + by) for i in range(length) if 0 <= i + by < length]
    return lax.ppermute(value, axis, pairs)


def gelu_slope(values):
    return jax.jvp(jax.nn.gelu, (values,), (jnp.ones_like(values),))[1]


def contract_first(left, right):
    return lax.dot_general(
        left, right, (((0,), (0,)), ((), ())), preferred_element_type=jnp.float32
    )


def contract_last(left, right):
    return lax.dot_general(
        left, right, (((1,), (1,)), ((), ())), preferred_element_type=jnp.float32
    )


def hop_steps(activations, dilation):
    return dilation // activations.shape[1]


def residual_block_forward(activations, conv_weight, point_weight, dilation):
    hop_count = hop_steps(activations, dilation)
    squash_part = jax.nn.gelu(activations.astype(jnp.float32)).astype(jnp.bfloat16)
    squashed = lax.all_gather(squash_part, "mp", axis=0, tiled=True)
    earlier = shifted(squashed, "ctx", hop_count)
    later = shifted(squashed, "ctx", -hop_count)
    pre_act = jnp.dot(conv_weight[0], earlier, preferred_element_type=jnp.float32)
    pre_act = pre_act + jnp.dot(conv_weight[1], squashed, preferred_element_type=jnp.float32)
    pre_act = pre_act + jnp.dot(conv_weight[2], later, preferred_element_type=jnp.float32)
    hidden = jax.nn.gelu(pre_act).astype(jnp.bfloat16)
    mixed = lax.psum_scatter(
        jnp.dot(point_weight, hidden, preferred_element_type=jnp.float32).astype(jnp.bfloat16),
        "mp",
        scatter_dimension=0,
        tiled=True,
    ).astype(jnp.float32)
    result = (activations.astype(jnp.float32) + mixed).astype(jnp.bfloat16)
    return (result, squashed, pre_act, hidden)


def residual_block_backward(
    incoming_gradient, activations, squashed, pre_act, hidden, conv_weight, point_weight, dilation
):
    hop_count = hop_steps(activations, dilation)
    upstream_full = lax.all_gather(incoming_gradient, "mp", axis=0, tiled=True)
    grad_hidden = contract_first(point_weight, upstream_full)
    grad_pre = (grad_hidden * gelu_slope(pre_act)).astype(jnp.bfloat16)
    grad_later = shifted(grad_pre, "ctx", -hop_count)
    grad_earlier = shifted(grad_pre, "ctx", hop_count)
    moved = (grad_later, grad_pre, grad_earlier)
    grad_conv = jnp.stack(
        [
            contract_last(moved[0], squashed),
            contract_last(moved[1], squashed),
            contract_last(moved[2], squashed),
        ]
    )
    grad_point = contract_last(upstream_full, hidden)
    total = contract_first(conv_weight[0], moved[0])
    total = total + contract_first(conv_weight[1], moved[1])
    grad_squash = lax.psum_scatter(
        (total + contract_first(conv_weight[2], moved[2])).astype(jnp.bfloat16),
        "mp",
        scatter_dimension=0,
        tiled=True,
    ).astype(jnp.float32)
    previous = (
        incoming_gradient.astype(jnp.float32)
        + grad_squash * gelu_slope(activations.astype(jnp.float32))
    ).astype(jnp.bfloat16)
    return (previous, grad_conv, grad_point)


def reduce_block(grad_conv, grad_point):
    return (
        lax.psum_scatter(
            grad_conv.astype(jnp.bfloat16), "ctx", scatter_dimension=2, tiled=True
        ).astype(jnp.float32),
        lax.psum_scatter(
            grad_point.astype(jnp.bfloat16), "ctx", scatter_dimension=0, tiled=True
        ).astype(jnp.float32),
    )


def shards(
    block_entry_input,
    first_conv_taps,
    first_pointwise_weight,
    second_conv_taps,
    second_pointwise_weight,
    grad_heads,
):
    regrouped = lax.all_to_all(grad_heads, "ctx", split_axis=2, concat_axis=1, tiled=True)
    incoming_gradient = regrouped.reshape(
        regrouped.shape[0] * regrouped.shape[1], regrouped.shape[2]
    )
    between_blocks_state, first_gelu_output, first_preactivation, first_hidden_state = (
        residual_block_forward(
            block_entry_input, first_conv_taps, first_pointwise_weight, FIRST_DILATION
        )
    )
    second_block_output, second_gelu_output, second_preactivation, second_hidden_state = (
        residual_block_forward(
            between_blocks_state, second_conv_taps, second_pointwise_weight, SECOND_DILATION
        )
    )
    incoming_gradient, conv_grad_b, point_grad_b = residual_block_backward(
        incoming_gradient,
        between_blocks_state,
        second_gelu_output,
        second_preactivation,
        second_hidden_state,
        second_conv_taps,
        second_pointwise_weight,
        SECOND_DILATION,
    )
    conv_grad_b, point_grad_b = reduce_block(conv_grad_b, point_grad_b)
    entry_input_gradient, conv_grad_a, point_grad_a = residual_block_backward(
        incoming_gradient,
        block_entry_input,
        first_gelu_output,
        first_preactivation,
        first_hidden_state,
        first_conv_taps,
        first_pointwise_weight,
        FIRST_DILATION,
    )
    conv_grad_a, point_grad_a = reduce_block(conv_grad_a, point_grad_a)
    return (
        second_block_output,
        entry_input_gradient,
        conv_grad_a,
        point_grad_a,
        conv_grad_b,
        point_grad_b,
    )


GELU_SCALE = 0.7978845608028654
GELU_CUBIC = 0.044715


def gelu_of(s):
    return 0.5 * s * (1.0 + jnp.tanh(GELU_SCALE * (s + GELU_CUBIC * (s * s * s))))


def slope_of(s):
    t = jnp.tanh(GELU_SCALE * (s + GELU_CUBIC * (s * s * s)))
    inner = GELU_SCALE * (1.0 + 3.0 * GELU_CUBIC * (s * s))
    return 0.5 * (1.0 + t) + 0.5 * s * (1.0 - t * t) * inner


def whole_kernel(
    n,
    x_h, k1_h, p1_h, k2_h, p2_h, g_h,
    out_o, gx_o, gk1_o, gp1_o, gk2_o, gp2_o,
    x_v, mid_v, k1, p1, k2, p2, z1, z2, g2, g1, u1, u2, gh, v2, gu2,
    v_all, gu_all, z_rows, g_rows,
    rs_out, rs_in, part, from_left, from_right,
    send, recv, load,
):
    rows, bins = x_v.shape
    chans = z1.shape[0]
    heads, vals = g_h.shape[0], g_h.shape[1]
    c, m = lax.axis_index("ctx"), lax.axis_index("mp")
    sib = m + 1 - 2 * (m % 2)
    cross = (m + 2) % 4
    far = 3 - m
    f32, bf16 = jnp.float32, jnp.bfloat16
    counter = iter(range(send.shape[0]))
    sent = []

    def remote(src, dst, i, by=None, **device):
        return pltpu.make_async_remote_copy(
            src_ref=src,
            dst_ref=dst,
            send_sem=send.at[i if by is None else by],
            recv_sem=recv.at[i],
            device_id=device,
            device_id_type=pl.DeviceIdType.MESH,
        )

    def start(copy):
        copy.start()
        sent.append(copy)

    loads = [
        pltpu.make_async_copy(src, dst, load.at[i])
        for i, (src, dst) in enumerate(
            ((x_h, x_v), (k1_h.at[1], k1), (p1_h, p1), (p2_h, p2), (k2_h.at[1], k2))
        )
    ]
    for copy in loads:
        copy.start()

    def grad_rows(owner, h):
        return pl.ds(pl.multiple_of(h * vals * n + owner * vals, 16), vals)

    def grad_bins(owner):
        return pl.ds(pl.multiple_of(owner * bins, 128), bins)

    own_grad = [
        pltpu.make_async_copy(
            g_h.at[h, :, grad_bins(c)], g2.at[m, grad_rows(c, h), :], load.at[5 + h]
        )
        for h in range(heads)
    ]
    for copy in own_grad:
        copy.start()

    barrier = pltpu.get_barrier_semaphore()
    for k in range(1, n):
        pl.semaphore_signal(
            barrier, inc=1, device_id={"ctx": (c + k) % n}, device_id_type=pl.DeviceIdType.MESH
        )
    for peer in (sib, cross):
        pl.semaphore_signal(
            barrier, inc=1, device_id={"mp": peer}, device_id_type=pl.DeviceIdType.MESH
        )

    def pieces(buf):
        return [lambda b: buf.at[b]]

    def gather_start(views):
        ids = []
        for view in views:
            own = [next(counter) for _ in range(3)]
            start(remote(view(m), view(m), own[0], mp=cross))
            start(remote(view(m), view(m), own[1], mp=sib))
            ids.append(own)
        return ids

    def gather_forward(views, ids):
        for view, own in zip(views, ids):
            remote(view(cross), view(cross), own[0], mp=cross).wait_recv()
            start(remote(view(cross), view(cross), own[2], mp=sib))

    def gather_end(views, ids):
        for view, own in zip(views, ids):
            remote(view(sib), view(sib), own[1], mp=sib).wait_recv()
            remote(view(far), view(far), own[2], mp=sib).wait_recv()

    def push_start(source, target):
        ids = [next(counter) for _ in range(n)]
        for k in range(1, n):
            peer = (c + k) % n
            start(remote(source(peer), target(c), ids[k], ctx=peer))
        return ids

    def push_wait(target, ids):
        for k in range(1, n):
            origin = (c + n - k) % n
            remote(target(origin), target(origin), ids[k], ctx=origin).wait_recv()

    fan_ids = [next(counter) for _ in range(2 * n)]

    def fan_copy(target, origin, k, by, peer):
        return remote(target(origin), target(origin), fan_ids[k], by=fan_ids[by], ctx=peer)

    def fan_own(target, act):
        for k in range(1, n):
            peer = (c + k) % n
            relayed = ((peer == n - 1) & (c < n - 2)) | ((peer == 0) & (c > 1))

            @pl.when(jnp.logical_not(relayed))
            def _():
                act(fan_copy(target, c, k, k, peer))

    def fan_passed(target, act):
        for origin in range(n - 2):

            @pl.when(c == n - 2)
            def _():
                act(target, origin, n - 2 - origin, n - 1 - origin, n - 1)

        for origin in range(n - 1, 1, -1):

            @pl.when(c == 1)
            def _():
                act(target, origin, n + 1 - origin, n - origin, 0)

    def pass_on(target, origin, arrived, k, peer):
        fan_copy(target, origin, arrived, arrived, peer).wait_recv()
        fan_copy(target, origin, k, n + origin, peer).start()

    def pass_done(target, origin, arrived, k, peer):
        fan_copy(target, origin, k, n + origin, peer).wait_send()

    def fan_wait(target):
        for k in range(1, n):
            origin = (c + n - k) % n
            waited = ((c == n - 2) & (origin < n - 2)) | ((c == 1) & (origin > 1))

            @pl.when(jnp.logical_not(waited))
            def _():
                fan_copy(target, origin, k, k, origin).wait_recv()

    def pair_start(buf):
        ids = [next(counter) for _ in range(n)]
        for k in range(1, n):
            own = buf.at[(c + k) % n, half(m % 2), :]
            start(remote(own, own, ids[k], mp=sib))
        return ids

    def pair_end(buf, ids):
        for k in range(1, n):
            other = buf.at[(c + k) % n, half(1 - m % 2), :]
            remote(other, other, ids[k], mp=sib).wait_recv()

    def half(b):
        return pl.ds(pl.multiple_of(b * (rows // 2), 16), rows // 2)

    def quarter(b):
        return pl.ds(pl.multiple_of(b * (rows // 4), 16), rows // 4)

    def row_views(buf):
        def view_of(k):
            return lambda b: buf.at[(c + k) % n, quarter(b), :]

        return [view_of(k) for k in range(1, n)]

    def scatter_start(i, block_of):
        ids = [next(counter) for _ in range(3)]
        for slot, block in ((0, far), (1, sib)):
            rs_out[i, slot] = block_of(block).astype(bf16)
            start(remote(rs_out.at[i, slot], rs_in.at[i, slot], ids[slot], mp=sib))
        return ids

    def scatter_cross(i, ids, block_of):
        term = block_of(cross)
        remote(rs_out.at[i, 0], rs_in.at[i, 0], ids[0], mp=sib).wait_recv()
        rs_out[i, 2] = (term + rs_in[i, 0].astype(f32)).astype(bf16)
        start(remote(rs_out.at[i, 2], rs_in.at[i, 2], ids[2], mp=cross))

    def scatter_end(i, ids, block_of):
        term = block_of(m)
        remote(rs_out.at[i, 1], rs_in.at[i, 1], ids[1], mp=sib).wait_recv()
        term = term + rs_in[i, 1].astype(f32)
        remote(rs_out.at[i, 2], rs_in.at[i, 2], ids[2], mp=cross).wait_recv()
        return term + rs_in[i, 2].astype(f32)

    line_ids = [[(next(counter), next(counter)) for _ in range(n)] for _ in range(2)]

    def to_right(i, d):
        peer = jnp.minimum(c + 1, n - 1)
        return remote(part.at[i, d], from_left.at[i, d], line_ids[i][d][0], ctx=peer)

    def to_left(i, d):
        peer = jnp.maximum(c - 1, 0)
        return remote(part.at[i, d], from_right.at[i, d], line_ids[i][d][1], ctx=peer)

    def line_first(*grads):
        for d in range(n - 1, 0, -1):
            for i in grads:

                @pl.when(c == 0)
                def _():
                    to_right(i, d).start()

                @pl.when(c == n - 1)
                def _():
                    to_left(i, n - 1 - d).start()

    def line_relay(i, hop):
        for d in range(n - 1, hop, -1):

            @pl.when(c == hop)
            def _():
                copy = to_right(i, d)
                copy.wait_recv()
                part[i, d] = (part[i, d].astype(f32) + from_left[i, d].astype(f32)).astype(bf16)
                copy.start()

            @pl.when(c == n - 1 - hop)
            def _():
                e = n - 1 - d
                copy = to_left(i, e)
                copy.wait_recv()
                part[i, e] = (part[i, e].astype(f32) + from_right[i, e].astype(f32)).astype(bf16)
                copy.start()

    def line_end(i, result):
        for d in range(n):

            @pl.when(c == d)
            def _():
                total = part[i, d].astype(f32)
                if d > 0:
                    to_right(i, d).wait_recv()
                    total = total + from_left[i, d].astype(f32)
                if d < n - 1:
                    to_left(i, d).wait_recv()
                    total = total + from_right[i, d].astype(f32)
                result[...] = total

    def line_drain(i):
        for d in range(n):

            @pl.when(c < d)
            def _():
                to_right(i, d).wait_send()

            @pl.when(c > d)
            def _():
                to_left(i, d).wait_send()

    def dot(a, b, left, right):
        return lax.dot_general(
            a, b, (((left,), (right,)), ((), ())), preferred_element_type=f32
        )

    def block_rows(b):
        return pl.ds(pl.multiple_of(b * rows, 128), rows)

    def mixed(p, v):
        return lambda b: dot(p[:, block_rows(b)], v[...], 0, 0)

    def spread(k, gu):
        return lambda b: dot(k[:, block_rows(b)], gu[...], 0, 0)

    def flat(buf):
        return buf[...].reshape(chans * rows, bins)

    def products(i, left, right):
        for d in range(n):
            part[i, d] = dot(left[...], right[d], 1, 1).astype(bf16)

    loads[0].wait()
    z1[m] = gelu_of(x_v[...].astype(f32)).astype(bf16)
    pl.semaphore_wait(barrier, n + 1)
    z1_ids = gather_start(pieces(z1))
    grad_ids = [[next(counter) for _ in range(heads)] for _ in range(n)]
    for k in range(1, n):
        peer = (c + k) % n
        for h in range(heads):
            start(
                remote(
                    g_h.at[h, :, grad_bins(peer)],
                    g2.at[m, grad_rows(c, h), :],
                    grad_ids[k][h],
                    ctx=peer,
                )
            )
    gather_forward(pieces(z1), z1_ids)
    for copy in loads[1:]:
        copy.wait()
    gather_end(pieces(z1), z1_ids)
    u1[...] = dot(k1[...], flat(z1), 1, 0)
    v_all[c] = gelu_of(u1[...]).astype(bf16)
    mixed1 = mixed(p1, v_all.at[c])
    rs_ids = scatter_start(0, mixed1)
    for copy in own_grad:
        copy.wait()
    for k in range(1, n):
        origin = (c + n - k) % n
        for h in range(heads):
            remote(
                g_h.at[h, :, grad_bins(origin)],
                g2.at[m, grad_rows(origin, h), :],
                grad_ids[k][h],
                ctx=origin,
            ).wait_recv()
    g2_ids = gather_start(pieces(g2))
    v_ids = push_start(lambda peer: v_all.at[c], lambda at: v_all.at[at])
    z_ids = push_start(
        lambda peer: z1.at[peer, half(m % 2), :], lambda at: z_rows.at[at, half(m % 2), :]
    )
    scatter_cross(0, rs_ids, mixed1)
    gather_forward(pieces(g2), g2_ids)
    middle = x_v[...].astype(f32) + scatter_end(0, rs_ids, mixed1)
    mid_v[...] = middle.astype(bf16)
    z2[m] = gelu_of(mid_v[...].astype(f32)).astype(bf16)
    z2_ids = gather_start(pieces(z2))
    gather_end(pieces(g2), g2_ids)
    gh[...] = dot(p2[...], flat(g2), 1, 0)
    gather_forward(pieces(z2), z2_ids)
    gather_end(pieces(z2), z2_ids)
    u2[...] = dot(k2[...], flat(z2), 1, 0)
    v2[...] = gelu_of(u2[...]).astype(bf16)
    gu2[...] = (gh[...] * slope_of(u2[...])).astype(bf16)
    spread2 = spread(k2, gu2)
    rs_ids = scatter_start(1, spread2)
    products(0, v2, g2)
    products(1, gu2, z2)
    line_first(0, 1)
    scatter_cross(1, rs_ids, spread2)
    mid_slope = slope_of(mid_v[...].astype(f32))
    mixed2 = mixed(p2, v2)
    out_ids = scatter_start(2, mixed2)
    previous = g2[m].astype(f32) + scatter_end(1, rs_ids, spread2) * mid_slope
    g1[m] = previous.astype(bf16)
    g1_ids = gather_start(pieces(g1))
    push_wait(lambda at: z_rows.at[at, half(m % 2), :], z_ids)
    z_row_ids = pair_start(z_rows)
    line_relay(0, 1)
    gather_forward(pieces(g1), g1_ids)
    gather_end(pieces(g1), g1_ids)
    g_ids = push_start(lambda peer: g1.at[peer, quarter(m), :], lambda at: g_rows.at[at, quarter(m), :])
    gh[...] = dot(p1[...], flat(g1), 1, 0)
    gu_all[c] = (gh[...] * slope_of(u1[...])).astype(bf16)
    fan_own(lambda at: gu_all.at[at], lambda copy: copy.start())
    spread1 = spread(k1, gu_all.at[c])
    rs_ids = scatter_start(3, spread1)
    line_relay(1, 1)
    scatter_cross(3, rs_ids, spread1)
    scatter_cross(2, out_ids, mixed2)
    for i in (0, 1):
        for hop in range(2, n - 1):
            line_relay(i, hop)
    push_wait(lambda at: g_rows.at[at, quarter(m), :], g_ids)
    g_row_ids = gather_start(row_views(g_rows))
    fan_passed(lambda at: gu_all.at[at], pass_on)
    first_slope = slope_of(x_v[...].astype(f32))
    previous = g1[m].astype(f32) + scatter_end(3, rs_ids, spread1) * first_slope
    gx_o[...] = previous.astype(bf16)
    result = mid_v[...].astype(f32) + scatter_end(2, out_ids, mixed2)
    out_o[...] = result.astype(bf16)
    gather_forward(row_views(g_rows), g_row_ids)
    pair_end(z_rows, z_row_ids)
    z_rows[c] = z1[c]
    g_rows[c] = g1[c]
    fan_wait(lambda at: gu_all.at[at])
    gk1_o[...] = sum(dot(gu_all[k], z_rows[k], 1, 1) for k in range(n))
    push_wait(lambda at: v_all.at[at], v_ids)
    gather_end(row_views(g_rows), g_row_ids)
    gp1_o[...] = sum(dot(v_all[k], g_rows[k], 1, 1) for k in range(n))
    for i, result_o in enumerate((gp2_o, gk2_o)):
        line_end(i, result_o)
    for copy in sent:
        copy.wait_send()
    fan_own(lambda at: gu_all.at[at], lambda copy: copy.wait_send())
    fan_passed(lambda at: gu_all.at[at], pass_done)
    for i in range(2):
        line_drain(i)


def write_results(
    out_i, gx_i, gk1_i, gp1_i, gk2_i, gp2_i, out_o, gx_o, gk1_o, gp1_o, gk2_o, gp2_o, zero, sems
):
    plain = [(gp1_i, gp1_o), (gp2_i, gp2_o), (gk1_i, gk1_o.at[1]), (gk2_i, gk2_o.at[1])]
    plain += [(out_i, out_o), (gx_i, gx_o)]
    copies = [pltpu.make_async_copy(src, dst, sems.at[i]) for i, (src, dst) in enumerate(plain)]
    for copy in copies:
        copy.start()
    zero[...] = jnp.zeros_like(zero)
    empty = [gk1_o.at[0], gk1_o.at[2], gk2_o.at[0], gk2_o.at[2]]
    fills = [pltpu.make_async_copy(zero, dst, sems.at[6 + i]) for i, dst in enumerate(empty)]
    for copy in fills:
        copy.start()
    for copy in copies + fills:
        copy.wait()


def short_sequence(sizes, x, k1, p1, k2, p2, grad):
    n, parts = sizes["ctx"], sizes["mp"]
    rows, bins = x.shape
    width = k1.shape[1]
    bf16, f32 = jnp.bfloat16, jnp.float32
    full = pltpu.VMEM((parts, rows, bins), bf16)
    shares = pltpu.VMEM((2, n, width, rows), bf16)
    copies = 24 + 4 * n + 6 * n + 3 * (n - 1) + grad.shape[0] * n
    inner = [pltpu.VMEM((width, bins), f32)] * 3 + [pltpu.VMEM((width, bins), bf16)] * 2
    results = pl.pallas_call(
        functools.partial(whole_kernel, n),
        out_shape=[
            jax.ShapeDtypeStruct((rows, bins), bf16),
            jax.ShapeDtypeStruct((rows, bins), bf16),
        ]
        + [jax.ShapeDtypeStruct((width, rows), f32)] * 4,
        in_specs=[pl.BlockSpec(memory_space=pl.ANY)] * 6,
        out_specs=[pl.BlockSpec(memory_space=pltpu.VMEM)] * 6,
        scratch_shapes=[
            pltpu.VMEM((rows, bins), bf16),
            pltpu.VMEM((rows, bins), bf16),
            pltpu.VMEM((width, k1.shape[2]), bf16),
            pltpu.VMEM(p1.shape[::-1], bf16),
            pltpu.VMEM((width, k1.shape[2]), bf16),
            pltpu.VMEM(p1.shape[::-1], bf16),
            full, full, full, full,
        ]
        + inner
        + [
            pltpu.VMEM((n, width, bins), bf16),
            pltpu.VMEM((n, width, bins), bf16),
            pltpu.VMEM((n, rows, bins), bf16),
            pltpu.VMEM((n, rows, bins), bf16),
            pltpu.VMEM((4, 3, rows, bins), bf16),
            pltpu.VMEM((4, 3, rows, bins), bf16),
            shares, shares, shares,
            pltpu.SemaphoreType.DMA((copies,)),
            pltpu.SemaphoreType.DMA((copies,)),
            pltpu.SemaphoreType.DMA((5 + grad.shape[0],)),
        ],
        compiler_params=pltpu.CompilerParams(
            collective_id=0, has_side_effects=True, vmem_limit_bytes=56 * 1024 * 1024
        ),
        name="blocks",
    )(x, k1, p1.T, k2, p2.T, grad)
    taps = jax.ShapeDtypeStruct((k1.shape[0], width, rows), f32)
    points = jax.ShapeDtypeStruct((width, rows), f32)
    out, gx, gk1, gp1, gk2, gp2 = pl.pallas_call(
        write_results,
        out_shape=[
            jax.ShapeDtypeStruct((rows, bins), bf16),
            jax.ShapeDtypeStruct((rows, bins), bf16),
            taps, points, taps, points,
        ],
        in_specs=[pl.BlockSpec(memory_space=pltpu.VMEM)] * 6,
        out_specs=[pl.BlockSpec(memory_space=pl.ANY)] * 6,
        scratch_shapes=[pltpu.VMEM((width, rows), f32), pltpu.SemaphoreType.DMA((10,))],
        name="results",
    )(*results)
    return out, gx, gk1, gp1.T, gk2, gp2.T


def device_program(sizes, x, k1, p1, k2, p2, grad):
    n = sizes["ctx"]
    length = n * x.shape[1]
    short = min(FIRST_DILATION, SECOND_DILATION) >= length
    if short and n == 4 and sizes["mp"] == 4:
        return short_sequence(sizes, x, k1, p1, k2, p2, grad)
    return shards(x, k1, p1, k2, p2, grad)


def solution(mesh):
    placed = (
        P("mp", ("groups", "ctx")),
        P(None, "mp", None),
        P(None, "mp"),
        P(None, "mp", None),
        P(None, "mp"),
        P("mp", "ctx", "groups"),
    )
    return jax.shard_map(
        functools.partial(device_program, dict(mesh.shape)),
        mesh=mesh,
        in_specs=placed,
        out_specs=(
            P("mp", ("groups", "ctx")),
            P("mp", ("groups", "ctx")),
            P("groups", "mp", "ctx"),
            P(("groups", "ctx"), "mp"),
            P("groups", "mp", "ctx"),
            P(("groups", "ctx"), "mp"),
        ),
        check_vma=False,
    )
```

```python
import functools

import jax
import jax.numpy as jnp
from jax import lax
from jax.experimental import pallas as pl
from jax.experimental.pallas import tpu as pltpu
from jax.sharding import PartitionSpec as P

FIRST_DILATION = 1024
SECOND_DILATION = 2048


def shifted(value, axis, by):
    length = lax.axis_size(axis)
    pairs = [(i, i + by) for i in range(length) if 0 <= i + by < length]
    return lax.ppermute(value, axis, pairs)


def gelu_slope(values):
    return jax.jvp(jax.nn.gelu, (values,), (jnp.ones_like(values),))[1]


def contract_first(left, right):
    return lax.dot_general(
        left, right, (((0,), (0,)), ((), ())), preferred_element_type=jnp.float32
    )


def contract_last(left, right):
    return lax.dot_general(
        left, right, (((1,), (1,)), ((), ())), preferred_element_type=jnp.float32
    )


def hop_steps(activations, dilation):
    return dilation // activations.shape[1]


def residual_block_forward(activations, conv_weight, point_weight, dilation):
    hop_count = hop_steps(activations, dilation)
    squash_part = jax.nn.gelu(activations.astype(jnp.float32)).astype(jnp.bfloat16)
    squashed = lax.all_gather(squash_part, "mp", axis=0, tiled=True)
    earlier = shifted(squashed, "ctx", hop_count)
    later = shifted(squashed, "ctx", -hop_count)
    pre_act = jnp.dot(conv_weight[0], earlier, preferred_element_type=jnp.float32)
    pre_act = pre_act + jnp.dot(conv_weight[1], squashed, preferred_element_type=jnp.float32)
    pre_act = pre_act + jnp.dot(conv_weight[2], later, preferred_element_type=jnp.float32)
    hidden = jax.nn.gelu(pre_act).astype(jnp.bfloat16)
    mixed = lax.psum_scatter(
        jnp.dot(point_weight, hidden, preferred_element_type=jnp.float32).astype(jnp.bfloat16),
        "mp",
        scatter_dimension=0,
        tiled=True,
    ).astype(jnp.float32)
    result = (activations.astype(jnp.float32) + mixed).astype(jnp.bfloat16)
    return (result, squashed, pre_act, hidden)


def residual_block_backward(
    incoming_gradient, activations, squashed, pre_act, hidden, conv_weight, point_weight, dilation
):
    hop_count = hop_steps(activations, dilation)
    upstream_full = lax.all_gather(incoming_gradient, "mp", axis=0, tiled=True)
    grad_hidden = contract_first(point_weight, upstream_full)
    grad_pre = (grad_hidden * gelu_slope(pre_act)).astype(jnp.bfloat16)
    grad_later = shifted(grad_pre, "ctx", -hop_count)
    grad_earlier = shifted(grad_pre, "ctx", hop_count)
    moved = (grad_later, grad_pre, grad_earlier)
    grad_conv = jnp.stack(
        [
            contract_last(moved[0], squashed),
            contract_last(moved[1], squashed),
            contract_last(moved[2], squashed),
        ]
    )
    grad_point = contract_last(upstream_full, hidden)
    total = contract_first(conv_weight[0], moved[0])
    total = total + contract_first(conv_weight[1], moved[1])
    grad_squash = lax.psum_scatter(
        (total + contract_first(conv_weight[2], moved[2])).astype(jnp.bfloat16),
        "mp",
        scatter_dimension=0,
        tiled=True,
    ).astype(jnp.float32)
    previous = (
        incoming_gradient.astype(jnp.float32)
        + grad_squash * gelu_slope(activations.astype(jnp.float32))
    ).astype(jnp.bfloat16)
    return (previous, grad_conv, grad_point)


def reduce_block(grad_conv, grad_point):
    return (
        lax.psum_scatter(
            grad_conv.astype(jnp.bfloat16), "ctx", scatter_dimension=2, tiled=True
        ).astype(jnp.float32),
        lax.psum_scatter(
            grad_point.astype(jnp.bfloat16), "ctx", scatter_dimension=0, tiled=True
        ).astype(jnp.float32),
    )


def shards(
    block_entry_input,
    first_conv_taps,
    first_pointwise_weight,
    second_conv_taps,
    second_pointwise_weight,
    grad_heads,
):
    regrouped = lax.all_to_all(grad_heads, "ctx", split_axis=2, concat_axis=1, tiled=True)
    incoming_gradient = regrouped.reshape(
        regrouped.shape[0] * regrouped.shape[1], regrouped.shape[2]
    )
    between_blocks_state, first_gelu_output, first_preactivation, first_hidden_state = (
        residual_block_forward(
            block_entry_input, first_conv_taps, first_pointwise_weight, FIRST_DILATION
        )
    )
    second_block_output, second_gelu_output, second_preactivation, second_hidden_state = (
        residual_block_forward(
            between_blocks_state, second_conv_taps, second_pointwise_weight, SECOND_DILATION
        )
    )
    incoming_gradient, conv_grad_b, point_grad_b = residual_block_backward(
        incoming_gradient,
        between_blocks_state,
        second_gelu_output,
        second_preactivation,
        second_hidden_state,
        second_conv_taps,
        second_pointwise_weight,
        SECOND_DILATION,
    )
    conv_grad_b, point_grad_b = reduce_block(conv_grad_b, point_grad_b)
    entry_input_gradient, conv_grad_a, point_grad_a = residual_block_backward(
        incoming_gradient,
        block_entry_input,
        first_gelu_output,
        first_preactivation,
        first_hidden_state,
        first_conv_taps,
        first_pointwise_weight,
        FIRST_DILATION,
    )
    conv_grad_a, point_grad_a = reduce_block(conv_grad_a, point_grad_a)
    return (
        second_block_output,
        entry_input_gradient,
        conv_grad_a,
        point_grad_a,
        conv_grad_b,
        point_grad_b,
    )


GELU_SCALE = 0.7978845608028654
GELU_CUBIC = 0.044715


def gelu_of(s):
    return 0.5 * s * (1.0 + jnp.tanh(GELU_SCALE * (s + GELU_CUBIC * (s * s * s))))


def slope_of(s):
    t = jnp.tanh(GELU_SCALE * (s + GELU_CUBIC * (s * s * s)))
    inner = GELU_SCALE * (1.0 + 3.0 * GELU_CUBIC * (s * s))
    return 0.5 * (1.0 + t) + 0.5 * s * (1.0 - t * t) * inner


def whole_kernel(
    n,
    x_h, k1_h, p1_h, k2_h, p2_h, g_h,
    out_o, gx_o, gk1_o, gp1_o, gk2_o, gp2_o,
    x_v, mid_v, k1, p1, k2, p2, z1, z2, g2, g1, u1, u2, gh, v2, gu2,
    v_all, gu_all, z_rows, g_rows,
    rs_out, rs_in, part, from_left, from_right,
    send, recv, load,
):
    rows, bins = x_v.shape
    chans = z1.shape[0]
    heads, vals = g_h.shape[0], g_h.shape[1]
    c, m = lax.axis_index("ctx"), lax.axis_index("mp")
    sib = m + 1 - 2 * (m % 2)
    cross = (m + 2) % 4
    far = 3 - m
    f32, bf16 = jnp.float32, jnp.bfloat16
    counter = iter(range(send.shape[0]))
    sent = []

    def remote(src, dst, i, by=None, **device):
        return pltpu.make_async_remote_copy(
            src_ref=src,
            dst_ref=dst,
            send_sem=send.at[i if by is None else by],
            recv_sem=recv.at[i],
            device_id=device,
            device_id_type=pl.DeviceIdType.MESH,
        )

    def start(copy):
        copy.start()
        sent.append(copy)

    loads = [
        pltpu.make_async_copy(src, dst, load.at[i])
        for i, (src, dst) in enumerate(
            ((x_h, x_v), (k1_h.at[1], k1), (p1_h, p1), (p2_h, p2), (k2_h.at[1], k2))
        )
    ]
    for copy in loads:
        copy.start()

    def grad_rows(owner, h):
        return pl.ds(pl.multiple_of(h * vals * n + owner * vals, 16), vals)

    def grad_bins(owner):
        return pl.ds(pl.multiple_of(owner * bins, 128), bins)

    own_grad = [
        pltpu.make_async_copy(
            g_h.at[h, :, grad_bins(c)], g2.at[m, grad_rows(c, h), :], load.at[5 + h]
        )
        for h in range(heads)
    ]
    for copy in own_grad:
        copy.start()

    barrier = pltpu.get_barrier_semaphore()
    for k in range(1, n):
        pl.semaphore_signal(
            barrier, inc=1, device_id={"ctx": (c + k) % n}, device_id_type=pl.DeviceIdType.MESH
        )
    for peer in (sib, cross):
        pl.semaphore_signal(
            barrier, inc=1, device_id={"mp": peer}, device_id_type=pl.DeviceIdType.MESH
        )

    def pieces(buf):
        return [lambda b: buf.at[b]]

    def gather_start(views):
        ids = []
        for view in views:
            own = [next(counter) for _ in range(3)]
            start(remote(view(m), view(m), own[0], mp=cross))
            start(remote(view(m), view(m), own[1], mp=sib))
            ids.append(own)
        return ids

    def gather_forward(views, ids):
        for view, own in zip(views, ids):
            remote(view(cross), view(cross), own[0], mp=cross).wait_recv()
            start(remote(view(cross), view(cross), own[2], mp=sib))

    def gather_end(views, ids):
        for view, own in zip(views, ids):
            remote(view(sib), view(sib), own[1], mp=sib).wait_recv()
            remote(view(far), view(far), own[2], mp=sib).wait_recv()

    def push_start(source, target):
        ids = [next(counter) for _ in range(n)]
        for k in range(1, n):
            peer = (c + k) % n
            start(remote(source(peer), target(c), ids[k], ctx=peer))
        return ids

    def push_wait(target, ids):
        for k in range(1, n):
            origin = (c + n - k) % n
            remote(target(origin), target(origin), ids[k], ctx=origin).wait_recv()

    fan_ids = [next(counter) for _ in range(2 * n)]

    def fan_copy(target, origin, k, by, peer):
        return remote(target(origin), target(origin), fan_ids[k], by=fan_ids[by], ctx=peer)

    def fan_own(target, act):
        for k in range(1, n):
            peer = (c + k) % n
            relayed = ((peer == n - 1) & (c < n - 2)) | ((peer == 0) & (c > 1))

            @pl.when(jnp.logical_not(relayed))
            def _():
                act(fan_copy(target, c, k, k, peer))

    def fan_passed(target, act):
        for origin in range(n - 2):

            @pl.when(c == n - 2)
            def _():
                act(target, origin, n - 2 - origin, n - 1 - origin, n - 1)

        for origin in range(n - 1, 1, -1):

            @pl.when(c == 1)
            def _():
                act(target, origin, n + 1 - origin, n - origin, 0)

    def pass_on(target, origin, arrived, k, peer):
        fan_copy(target, origin, arrived, arrived, peer).wait_recv()
        fan_copy(target, origin, k, n + origin, peer).start()

    def pass_done(target, origin, arrived, k, peer):
        fan_copy(target, origin, k, n + origin, peer).wait_send()

    def fan_wait(target):
        for k in range(1, n):
            origin = (c + n - k) % n
            waited = ((c == n - 2) & (origin < n - 2)) | ((c == 1) & (origin > 1))

            @pl.when(jnp.logical_not(waited))
            def _():
                fan_copy(target, origin, k, k, origin).wait_recv()

    def pair_start(buf):
        ids = [next(counter) for _ in range(n)]
        for k in range(1, n):
            own = buf.at[(c + k) % n, half(m % 2), :]
            start(remote(own, own, ids[k], mp=sib))
        return ids

    def pair_end(buf, ids):
        for k in range(1, n):
            other = buf.at[(c + k) % n, half(1 - m % 2), :]
            remote(other, other, ids[k], mp=sib).wait_recv()

    def half(b):
        return pl.ds(pl.multiple_of(b * (rows // 2), 16), rows // 2)

    def quarter(b):
        return pl.ds(pl.multiple_of(b * (rows // 4), 16), rows // 4)

    def row_views(buf):
        def view_of(k):
            return lambda b: buf.at[(c + k) % n, quarter(b), :]

        return [view_of(k) for k in range(1, n)]

    def scatter_start(i, block_of):
        ids = [next(counter) for _ in range(3)]
        for slot, block in ((0, far), (1, sib)):
            rs_out[i, slot] = block_of(block).astype(bf16)
            start(remote(rs_out.at[i, slot], rs_in.at[i, slot], ids[slot], mp=sib))
        return ids

    def scatter_cross(i, ids, block_of):
        term = block_of(cross)
        remote(rs_out.at[i, 0], rs_in.at[i, 0], ids[0], mp=sib).wait_recv()
        rs_out[i, 2] = (term + rs_in[i, 0].astype(f32)).astype(bf16)
        start(remote(rs_out.at[i, 2], rs_in.at[i, 2], ids[2], mp=cross))

    def scatter_end(i, ids, block_of):
        term = block_of(m)
        remote(rs_out.at[i, 1], rs_in.at[i, 1], ids[1], mp=sib).wait_recv()
        term = term + rs_in[i, 1].astype(f32)
        remote(rs_out.at[i, 2], rs_in.at[i, 2], ids[2], mp=cross).wait_recv()
        return term + rs_in[i, 2].astype(f32)

    line_ids = [[(next(counter), next(counter)) for _ in range(n)] for _ in range(2)]

    def to_right(i, d):
        peer = jnp.minimum(c + 1, n - 1)
        return remote(part.at[i, d], from_left.at[i, d], line_ids[i][d][0], ctx=peer)

    def to_left(i, d):
        peer = jnp.maximum(c - 1, 0)
        return remote(part.at[i, d], from_right.at[i, d], line_ids[i][d][1], ctx=peer)

    def line_first(*grads):
        for d in range(n - 1, 0, -1):
            for i in grads:

                @pl.when(c == 0)
                def _():
                    to_right(i, d).start()

                @pl.when(c == n - 1)
                def _():
                    to_left(i, n - 1 - d).start()

    def line_relay(i, hop):
        for d in range(n - 1, hop, -1):

            @pl.when(c == hop)
            def _():
                copy = to_right(i, d)
                copy.wait_recv()
                part[i, d] = (part[i, d].astype(f32) + from_left[i, d].astype(f32)).astype(bf16)
                copy.start()

            @pl.when(c == n - 1 - hop)
            def _():
                e = n - 1 - d
                copy = to_left(i, e)
                copy.wait_recv()
                part[i, e] = (part[i, e].astype(f32) + from_right[i, e].astype(f32)).astype(bf16)
                copy.start()

    def line_end(i, result):
        for d in range(n):

            @pl.when(c == d)
            def _():
                total = part[i, d].astype(f32)
                if d > 0:
                    to_right(i, d).wait_recv()
                    total = total + from_left[i, d].astype(f32)
                if d < n - 1:
                    to_left(i, d).wait_recv()
                    total = total + from_right[i, d].astype(f32)
                result[...] = total

    def line_drain(i):
        for d in range(n):

            @pl.when(c < d)
            def _():
                to_right(i, d).wait_send()

            @pl.when(c > d)
            def _():
                to_left(i, d).wait_send()

    def dot(a, b, left, right):
        return lax.dot_general(
            a, b, (((left,), (right,)), ((), ())), preferred_element_type=f32
        )

    def block_rows(b):
        return pl.ds(pl.multiple_of(b * rows, 128), rows)

    def mixed(p, v):
        return lambda b: dot(p[:, block_rows(b)], v[...], 0, 0)

    def spread(k, gu):
        return lambda b: dot(k[:, block_rows(b)], gu[...], 0, 0)

    def flat(buf):
        return buf[...].reshape(chans * rows, bins)

    def products(i, left, right):
        for d in range(n):
            part[i, d] = dot(left[...], right[d], 1, 1).astype(bf16)

    loads[0].wait()
    z1[m] = gelu_of(x_v[...].astype(f32)).astype(bf16)
    pl.semaphore_wait(barrier, n + 1)
    z1_ids = gather_start(pieces(z1))
    grad_ids = [[next(counter) for _ in range(heads)] for _ in range(n)]
    for k in range(1, n):
        peer = (c + k) % n
        for h in range(heads):
            start(
                remote(
                    g_h.at[h, :, grad_bins(peer)],
                    g2.at[m, grad_rows(c, h), :],
                    grad_ids[k][h],
                    ctx=peer,
                )
            )
    gather_forward(pieces(z1), z1_ids)
    for copy in loads[1:]:
        copy.wait()
    gather_end(pieces(z1), z1_ids)
    u1[...] = dot(k1[...], flat(z1), 1, 0)
    v_all[c] = gelu_of(u1[...]).astype(bf16)
    mixed1 = mixed(p1, v_all.at[c])
    rs_ids = scatter_start(0, mixed1)
    for copy in own_grad:
        copy.wait()
    for k in range(1, n):
        origin = (c + n - k) % n
        for h in range(heads):
            remote(
                g_h.at[h, :, grad_bins(origin)],
                g2.at[m, grad_rows(origin, h), :],
                grad_ids[k][h],
                ctx=origin,
            ).wait_recv()
    g2_ids = gather_start(pieces(g2))
    v_ids = push_start(lambda peer: v_all.at[c], lambda at: v_all.at[at])
    z_ids = push_start(
        lambda peer: z1.at[peer, half(m % 2), :], lambda at: z_rows.at[at, half(m % 2), :]
    )
    scatter_cross(0, rs_ids, mixed1)
    gather_forward(pieces(g2), g2_ids)
    middle = x_v[...].astype(f32) + scatter_end(0, rs_ids, mixed1)
    mid_v[...] = middle.astype(bf16)
    z2[m] = gelu_of(mid_v[...].astype(f32)).astype(bf16)
    z2_ids = gather_start(pieces(z2))
    gather_end(pieces(g2), g2_ids)
    gh[...] = dot(p2[...], flat(g2), 1, 0)
    gather_forward(pieces(z2), z2_ids)
    gather_end(pieces(z2), z2_ids)
    u2[...] = dot(k2[...], flat(z2), 1, 0)
    v2[...] = gelu_of(u2[...]).astype(bf16)
    gu2[...] = (gh[...] * slope_of(u2[...])).astype(bf16)
    spread2 = spread(k2, gu2)
    rs_ids = scatter_start(1, spread2)
    products(0, v2, g2)
    products(1, gu2, z2)
    line_first(0, 1)
    scatter_cross(1, rs_ids, spread2)
    mid_slope = slope_of(mid_v[...].astype(f32))
    mixed2 = mixed(p2, v2)
    out_ids = scatter_start(2, mixed2)
    previous = g2[m].astype(f32) + scatter_end(1, rs_ids, spread2) * mid_slope
    g1[m] = previous.astype(bf16)
    g1_ids = gather_start(pieces(g1))
    gather_forward(pieces(g1), g1_ids)
    push_wait(lambda at: z_rows.at[at, half(m % 2), :], z_ids)
    z_row_ids = pair_start(z_rows)
    line_relay(0, 1)
    gather_end(pieces(g1), g1_ids)
    g_ids = push_start(lambda peer: g1.at[peer, quarter(m), :], lambda at: g_rows.at[at, quarter(m), :])
    gh[...] = dot(p1[...], flat(g1), 1, 0)
    gu_all[c] = (gh[...] * slope_of(u1[...])).astype(bf16)
    fan_own(lambda at: gu_all.at[at], lambda copy: copy.start())
    spread1 = spread(k1, gu_all.at[c])
    rs_ids = scatter_start(3, spread1)
    line_relay(1, 1)
    scatter_cross(3, rs_ids, spread1)
    scatter_cross(2, out_ids, mixed2)
    for i in (0, 1):
        for hop in range(2, n - 1):
            line_relay(i, hop)
    push_wait(lambda at: g_rows.at[at, quarter(m), :], g_ids)
    g_row_ids = gather_start(row_views(g_rows))
    fan_passed(lambda at: gu_all.at[at], pass_on)
    first_slope = slope_of(x_v[...].astype(f32))
    previous = g1[m].astype(f32) + scatter_end(3, rs_ids, spread1) * first_slope
    gx_o[...] = previous.astype(bf16)
    result = mid_v[...].astype(f32) + scatter_end(2, out_ids, mixed2)
    out_o[...] = result.astype(bf16)
    gather_forward(row_views(g_rows), g_row_ids)
    pair_end(z_rows, z_row_ids)
    z_rows[c] = z1[c]
    g_rows[c] = g1[c]
    fan_wait(lambda at: gu_all.at[at])
    gk1_o[...] = sum(dot(gu_all[k], z_rows[k], 1, 1) for k in range(n))
    push_wait(lambda at: v_all.at[at], v_ids)
    gather_end(row_views(g_rows), g_row_ids)
    gp1_o[...] = sum(dot(v_all[k], g_rows[k], 1, 1) for k in range(n))
    for i, result_o in enumerate((gp2_o, gk2_o)):
        line_end(i, result_o)
    for copy in sent:
        copy.wait_send()
    fan_own(lambda at: gu_all.at[at], lambda copy: copy.wait_send())
    fan_passed(lambda at: gu_all.at[at], pass_done)
    for i in range(2):
        line_drain(i)


def write_results(
    out_i, gx_i, gk1_i, gp1_i, gk2_i, gp2_i, out_o, gx_o, gk1_o, gp1_o, gk2_o, gp2_o, zero, sems
):
    plain = [(gp1_i, gp1_o), (gp2_i, gp2_o), (gk1_i, gk1_o.at[1]), (gk2_i, gk2_o.at[1])]
    plain += [(out_i, out_o), (gx_i, gx_o)]
    copies = [pltpu.make_async_copy(src, dst, sems.at[i]) for i, (src, dst) in enumerate(plain)]
    for copy in copies:
        copy.start()
    zero[...] = jnp.zeros_like(zero)
    empty = [gk1_o.at[0], gk1_o.at[2], gk2_o.at[0], gk2_o.at[2]]
    fills = [pltpu.make_async_copy(zero, dst, sems.at[6 + i]) for i, dst in enumerate(empty)]
    for copy in fills:
        copy.start()
    for copy in copies + fills:
        copy.wait()


def short_sequence(sizes, x, k1, p1, k2, p2, grad):
    n, parts = sizes["ctx"], sizes["mp"]
    rows, bins = x.shape
    width = k1.shape[1]
    bf16, f32 = jnp.bfloat16, jnp.float32
    full = pltpu.VMEM((parts, rows, bins), bf16)
    shares = pltpu.VMEM((2, n, width, rows), bf16)
    copies = 24 + 4 * n + 6 * n + 3 * (n - 1) + grad.shape[0] * n
    inner = [pltpu.VMEM((width, bins), f32)] * 3 + [pltpu.VMEM((width, bins), bf16)] * 2
    results = pl.pallas_call(
        functools.partial(whole_kernel, n),
        out_shape=[
            jax.ShapeDtypeStruct((rows, bins), bf16),
            jax.ShapeDtypeStruct((rows, bins), bf16),
        ]
        + [jax.ShapeDtypeStruct((width, rows), f32)] * 4,
        in_specs=[pl.BlockSpec(memory_space=pl.ANY)] * 6,
        out_specs=[pl.BlockSpec(memory_space=pltpu.VMEM)] * 6,
        scratch_shapes=[
            pltpu.VMEM((rows, bins), bf16),
            pltpu.VMEM((rows, bins), bf16),
            pltpu.VMEM((width, k1.shape[2]), bf16),
            pltpu.VMEM(p1.shape[::-1], bf16),
            pltpu.VMEM((width, k1.shape[2]), bf16),
            pltpu.VMEM(p1.shape[::-1], bf16),
            full, full, full, full,
        ]
        + inner
        + [
            pltpu.VMEM((n, width, bins), bf16),
            pltpu.VMEM((n, width, bins), bf16),
            pltpu.VMEM((n, rows, bins), bf16),
            pltpu.VMEM((n, rows, bins), bf16),
            pltpu.VMEM((4, 3, rows, bins), bf16),
            pltpu.VMEM((4, 3, rows, bins), bf16),
            shares, shares, shares,
            pltpu.SemaphoreType.DMA((copies,)),
            pltpu.SemaphoreType.DMA((copies,)),
            pltpu.SemaphoreType.DMA((5 + grad.shape[0],)),
        ],
        compiler_params=pltpu.CompilerParams(
            collective_id=0, has_side_effects=True, vmem_limit_bytes=56 * 1024 * 1024
        ),
        name="blocks",
    )(x, k1, p1.T, k2, p2.T, grad)
    taps = jax.ShapeDtypeStruct((k1.shape[0], width, rows), f32)
    points = jax.ShapeDtypeStruct((width, rows), f32)
    out, gx, gk1, gp1, gk2, gp2 = pl.pallas_call(
        write_results,
        out_shape=[
            jax.ShapeDtypeStruct((rows, bins), bf16),
            jax.ShapeDtypeStruct((rows, bins), bf16),
            taps, points, taps, points,
        ],
        in_specs=[pl.BlockSpec(memory_space=pl.ANY)] * 6,
        out_specs=[pl.BlockSpec(memory_space=pl.ANY)] * 6,
        scratch_shapes=[pltpu.VMEM((width, rows), f32), pltpu.SemaphoreType.DMA((10,))],
        name="results",
    )(*results)
    return out, gx, gk1, gp1.T, gk2, gp2.T


def device_program(sizes, x, k1, p1, k2, p2, grad):
    n = sizes["ctx"]
    length = n * x.shape[1]
    short = min(FIRST_DILATION, SECOND_DILATION) >= length
    if short and n == 4 and sizes["mp"] == 4:
        return short_sequence(sizes, x, k1, p1, k2, p2, grad)
    return shards(x, k1, p1, k2, p2, grad)


def solution(mesh):
    placed = (
        P("mp", ("groups", "ctx")),
        P(None, "mp", None),
        P(None, "mp"),
        P(None, "mp", None),
        P(None, "mp"),
        P("mp", "ctx", "groups"),
    )
    return jax.shard_map(
        functools.partial(device_program, dict(mesh.shape)),
        mesh=mesh,
        in_specs=placed,
        out_specs=(
            P("mp", ("groups", "ctx")),
            P("mp", ("groups", "ctx")),
            P("groups", "mp", "ctx"),
            P(("groups", "ctx"), "mp"),
            P("groups", "mp", "ctx"),
            P(("groups", "ctx"), "mp"),
        ),
        check_vma=False,
    )
```
